32 devices in a mesh: groups: 2 (over y), rep: 4 (over z), head: 4 (over x, core).
Axes of the slice: x: 2, y: 2, z: 4, core: 2. Of those that a mesh axis runs over, the one named last changes fastest.
Arguments:
- residual: bfloat16 [32, 5120], P(('groups', 'rep'), 'head'), parts along dimension 0, may hold values from -3 to 3
- queries: bfloat16 [32, 96, 128], P(('groups', 'rep'), 'head'), parts along dimension 0, may hold values from -110 to 110
- cache_keys: bfloat16 [32, 8, 128, 128], P(('groups', 'rep'), 'head'), parts along dimension 0, may hold values from -5 to 5
- cache_values: bfloat16 [32, 8, 128, 128], P(('groups', 'rep'), 'head'), parts along dimension 0, may hold values from -5 to 5
- new_keys: bfloat16 [32, 8, 128], P(('groups', 'rep'), 'head'), parts along dimension 0, may hold values from -5 to 5
- new_values: bfloat16 [32, 8, 128], P(('groups', 'rep'), 'head'), parts along dimension 0, may hold values from -5 to 5
- cache_lengths: int32 [32], P(('groups', 'rep')), parts along dimension 0, may hold values from 1 to 128, as said below
- out_proj: bfloat16 [12288, 5120], P('head', 'rep'), may hold values from -0.21875 to 0.21875
- norm_gain: float32 [5120], replicated, may hold values from 0.25 to 2.5
- skip_flags: int32 [32], P(('groups', 'rep')), parts along dimension 0, may hold values 0 or 1
- expert_ids: int32 [32, 2], P(('groups', 'rep')), parts along dimension 0, may hold values from 0 to 3, all different within a row; in each aligned block of 4 rows (0 to 3, 4 to 7, ...) at most 2 rows name the same one
- route_scores: float32 [32, 2], P(('groups', 'rep')), parts along dimension 0, may hold values from 0.05 to 1
- gate_w: bfloat16 [4, 5120, 1024], P('rep', None, 'head'), may hold values from -0.078125 to 0.078125
- up_w: bfloat16 [4, 5120, 1024], P('rep', None, 'head'), may hold values from -0.078125 to 0.078125
- down_w: bfloat16 [4, 1024, 5120], P('rep', 'head'), may hold values from -0.1875 to 0.1875
Outputs:
- layer_out: bfloat16 [32, 5120], P(('groups', 'rep'), 'head'), parts along dimension 0
The draws below stay inside these ranges and needn't reach their ends.
There are 2 independent parts, one for each index of `groups`. The reference program is written for one: setup_inputs(seed, part) draws one part's arguments, and reference() takes and returns one part's arrays. A program takes and returns all parts, laid end to end along the dimension named above; an argument that names none is the same for every part. Nothing has to cross between parts.
Inputs may be any that keep to these rules, and one draw needn't show every extreme that they name: `cache_lengths`: number of filled cache slots of each row; in every aligned block of 4 rows one row has all 128. `skip_flags`: 1 marks a row that skips the layer. `expert_ids`: each row names 2 different experts; among the 4 rows of one device no expert is named by more than 2 rows, a bound that some block reaches.
All inputs are finite; a program needn't handle non-finite values. No bound on the sum of `skip_flags` on one device may be relied on, other than what follows from the above.
Results may differ from the reference program's by a relative error of at most 0.018.
Values may be sent and summed in bfloat16 or wider, within the bound.
A program may use at most 64 MiB of HBM per device.

```python
import math
import jax
import jax.numpy as jnp
import numpy as np
from jax import lax

D = 5120
QH = 96
KVH = 8
HD = 128
FFW = 1024
CACHE = 128
ROW_DEV = 4
EXPERTS = 4
TOPK = 2
CAP = 2
ROWS = 16
N_REP = 4


def base_keys(key):
    return jnp.clip(jax.random.normal(key, (ROWS, KVH, CACHE, HD), jnp.float32), -5.0, 5.0)


def draw_cache_keys(key, part):
    shared = base_keys(key)
    return shared.astype(jnp.bfloat16)


def draw_queries(key, part):
    key = jax.random.fold_in(key, 12)
    entries = jnp.clip(jax.random.normal(key, (ROWS, QH, HD), jnp.float32), -5.0, 5.0)
    return entries.astype(jnp.bfloat16)


def draw_cache_lengths(key, part):
    key = jax.random.fold_in(key, 13)
    first_key, second_key = jax.random.split(key)
    drawn = jax.random.randint(first_key, (ROWS,), 1, CACHE + 1, dtype=jnp.int32)
    chosen = jax.random.randint(second_key, (ROWS // ROW_DEV,), 0, ROW_DEV, dtype=jnp.int32)
    marked = jnp.arange(ROWS, dtype=jnp.int32) % ROW_DEV == jnp.repeat(chosen, ROW_DEV)
    return jnp.where(marked, CACHE, drawn).astype(jnp.int32)


def place_ends(array, rng, low, largest):
    place = [jax.random.randint(jax.random.fold_in(rng, axis), (), 0, length) for axis, length in enumerate(array.shape)]
    widest = array.shape.index(max(array.shape))
    next_to = place[:widest] + [(place[widest] + 1) % array.shape[widest]] + place[widest + 1:]
    return array.at[tuple(place)].set(low).at[tuple(next_to)].set(largest)


def block_levels(rng, shape, cuts, smallest, high):
    factor_of = 1.0
    for position, blocks in cuts:
        draws = jax.random.uniform(jax.random.fold_in(jax.random.fold_in(rng, 6), position), (blocks,), jnp.float32, smallest / len(cuts), high / len(cuts))
        factor_of = factor_of * jnp.repeat(jnp.exp(draws), shape[position] // blocks).reshape((-1,) + (1,) * (len(shape) - 1 - position))
    return factor_of


def assign_block(key, own, number, rows, amount, top, reach, skew):
    ranking = jax.random.permutation(key, amount)
    crowded, ordinary = portions_of(amount, rows * top, reach, skew, True), portions_of(amount, rows * top, reach, skew, False)
    places = jnp.arange(amount)

    def named(tallies, turn):
        used = int((tallies > 0).sum())
        fixed = max(1, used // 4)
        moved = fixed + (places - fixed + turn * (used - fixed)) % max(1, amount - fixed)
        return jnp.zeros((amount,), jnp.int32).at[ranking[jnp.where(places < fixed, places, moved)]].set(jnp.asarray(tallies, jnp.int32))

    tallies = jnp.where(number % 4 == 0, named(crowded, number // 4), named(ordinary, number - number // 4 - 1))
    mixed = jax.random.permutation(jax.random.fold_in(own, 3), amount)
    source_of, receiver = mixed[0:amount // 2 * 2:2], mixed[1:amount // 2 * 2:2]
    margin = jnp.minimum(tallies[source_of] - 1, reach - tallies[receiver]) // 2
    margin = jnp.where((source_of == ranking[0]) | (receiver == ranking[0]) | (tallies[receiver] == 0), 0, jnp.maximum(margin, 0))
    moved = jax.random.randint(jax.random.fold_in(own, 4), (amount // 2,), 0, 1 << 20) % (margin + 1)
    tallies = tallies.at[source_of].add(-moved).at[receiver].add(moved)
    items = jnp.searchsorted(jnp.cumsum(tallies), jnp.arange(rows * top), side="right").astype(jnp.int32)
    grid = items.reshape(top, rows).T
    grid = grid[jax.random.permutation(jax.random.fold_in(own, 1), rows)]
    turn = jax.random.randint(jax.random.fold_in(own, 2), (rows, 1), 0, top)
    return jnp.take_along_axis(grid, (jnp.arange(top)[None, :] + turn) % top, axis=1)


def portions_of(count, total, most, skew, full):
    loads = [(1 << 20) // math.isqrt(standing ** skew) + 1 for standing in range(1, count + 1)]
    largest = most if full else min(most, max(-(-total // count), total * loads[0] // sum(loads)))
    least = 1 if total - largest >= count - 1 else 0
    given, surplus = [largest] + [least] * (count - 1), total - largest - least * (count - 1)
    while surplus > 0:
        free = [i for i in range(1, count) if given[i] < largest] or [i for i in range(1, count) if given[i] < most]
        mass, left = sum([loads[i] for i in free]), surplus
        for i in free:
            extra = min(most - given[i], max(1, left * loads[i] // mass), surplus)
            given[i] = given[i] + extra
            surplus = surplus - extra
    return np.array(given)


def gaussian(stream_key, dims, deviation, most, cuts=(), kind=jnp.bfloat16):
    values = deviation * jax.random.normal(stream_key, dims, jnp.float32)
    if cuts:
        values = values * block_levels(stream_key, dims, cuts, -0.22, 0.18)
    return jnp.clip(values, -most, most).astype(kind)


def setup_inputs(seed: int = 0, part: int = 0) -> dict:
    key_list = jax.random.split(jax.random.key(seed), 16)
    part_splits = jax.random.split(jax.random.fold_in(key_list[15], part), 16)
    residual = gaussian(part_splits[0], (ROWS, D), 0.5, 3.0, ((0, 4), (1, 4)))
    queries = draw_queries(jax.random.fold_in(jax.random.fold_in(key_list[15], part), 71), part)
    cache_keys = draw_cache_keys(jax.random.fold_in(jax.random.fold_in(key_list[15], part), 71), part)
    cache_values = gaussian(part_splits[3], (ROWS, KVH, CACHE, HD), 1.0, 5.0, ((0, 4), (1, 4)))
    new_keys = gaussian(part_splits[4], (ROWS, KVH, HD), 1.0, 5.0, ((0, 4), (1, 4)))
    new_values = gaussian(part_splits[5], (ROWS, KVH, HD), 1.0, 5.0, ((0, 4), (1, 4)))
    cache_lengths = draw_cache_lengths(jax.random.fold_in(jax.random.fold_in(key_list[15], part), 71), part)
    out_proj = gaussian(key_list[7], (QH * HD, D), (QH * HD // 16) ** -0.5, 0.21875, ((0, 4), (1, 4)))
    norm_gain = jnp.clip(jnp.exp(jax.random.uniform(key_list[8], (D,), jnp.float32, math.log(0.25), math.log(2.5))), 0.25, 2.5)
    skip_flags = place_ends((jax.random.randint(part_splits[9], (ROWS,), 0, 8) < 1).astype(jnp.int32), jax.random.fold_in(part_splits[9], 1), 0, 1)
    expert_ids_keys = jax.random.split(jax.random.fold_in(part_splits[10], 1), ROWS // ROW_DEV)
    expert_ids_turns = jax.random.permutation(jax.random.fold_in(part_splits[10], 3), ROWS // ROW_DEV)
    expert_ids = jax.vmap(lambda own, number: assign_block(jax.random.fold_in(part_splits[10], 2), own, number, ROW_DEV, EXPERTS, TOPK, CAP, 2))(expert_ids_keys, expert_ids_turns).reshape((ROWS, TOPK))
    route_scores = jnp.clip(jnp.exp(math.log(1.0) - 2.9957323 * jax.random.uniform(part_splits[11], (ROWS, TOPK), jnp.float32) ** block_levels(part_splits[11], (ROWS, TOPK), ((0, 4),), -0.2, 0.2)), 0.05, 1.0)
    gate_w = gaussian(key_list[12], (EXPERTS, D, FFW), D ** -0.5, 0.078125, ((0, 4), (2, 4)))
    up_w = gaussian(key_list[13], (EXPERTS, D, FFW), D ** -0.5, 0.078125, ((0, 4), (2, 4)))
    down_w = gaussian(key_list[14], (EXPERTS, FFW, D), FFW ** -0.5, 0.1875, ((0, 4), (1, 4)))
    return {"residual": residual, "queries": queries, "cache_keys": cache_keys, "cache_values": cache_values, "new_keys": new_keys, "new_values": new_values, "cache_lengths": cache_lengths, "out_proj": out_proj, "norm_gain": norm_gain, "skip_flags": skip_flags, "expert_ids": expert_ids, "route_scores": route_scores, "gate_w": gate_w, "up_w": up_w, "down_w": down_w}


def reference(residual, queries, cache_keys, cache_values, new_keys, new_values, cache_lengths, out_proj, norm_gain, skip_flags, expert_ids, route_scores, gate_w, up_w, down_w):
    row_total = residual.shape[0]
    group_size = QH // KVH
    scaling = 1.0 / math.sqrt(HD)
    grouped = queries.astype(jnp.float32).reshape(row_total, KVH, group_size, HD)
    scores = jnp.einsum('rkgd,rkpd->rkgp', grouped, cache_keys.astype(jnp.float32)) * scaling
    own_score = jnp.einsum('rkgd,rkd->rkg', grouped, new_keys.astype(jnp.float32)) * scaling
    filled = jnp.arange(CACHE, dtype=jnp.int32)[None, :] < cache_lengths[:, None]
    scores = jnp.where(filled[:, None, None, :], scores, -jnp.inf)
    highest = jnp.maximum(lax.optimization_barrier(jnp.max(scores, axis=-1)), own_score)
    powers = jnp.exp(scores - highest[..., None])
    own_power = jnp.exp(own_score - highest)
    denominator = lax.optimization_barrier(jnp.sum(powers, axis=-1)) + own_power
    probs = (powers / denominator[..., None]).astype(jnp.bfloat16)
    own_prob = (own_power / denominator).astype(jnp.bfloat16)
    attended = jnp.einsum('rkgp,rkpd->rkgd', probs.astype(jnp.float32), cache_values.astype(jnp.float32))
    attended = attended + own_prob.astype(jnp.float32)[..., None] * new_values.astype(jnp.float32)[:, :, None, :]
    attended = attended.astype(jnp.bfloat16).reshape(row_total, QH * HD)
    projected = jnp.dot(attended, out_proj, preferred_element_type=jnp.float32)
    middle = (residual.astype(jnp.float32) + projected).astype(jnp.bfloat16)
    middle_wide = middle.astype(jnp.float32)
    mean_square = lax.optimization_barrier(jnp.mean(middle_wide * middle_wide, axis=-1, keepdims=True))
    normed = (middle_wide * lax.rsqrt(mean_square + 1e-05) * norm_gain[None, :]).astype(jnp.bfloat16)
    live = skip_flags == 0
    expert_range = jnp.arange(EXPERTS, dtype=jnp.int32)
    choose = ((expert_ids[:, :, None] == expert_range[None, None, :]) & live[:, None, None]).astype(jnp.int32)
    per_device = choose.reshape(N_REP, ROW_DEV * TOPK, EXPERTS)
    before = jnp.cumsum(per_device, axis=1) - per_device
    rank = lax.optimization_barrier(jnp.sum(before * per_device, axis=-1)).reshape(row_total, TOPK)
    bucket = N_REP * CAP
    source = (jnp.arange(row_total, dtype=jnp.int32) // ROW_DEV)[:, None]
    slot = expert_ids * bucket + source * CAP + rank
    slot = jnp.where(live[:, None], slot, EXPERTS * bucket).astype(jnp.int32)
    row_index = jnp.broadcast_to(jnp.arange(row_total, dtype=jnp.int32)[:, None], (row_total, TOPK))
    table = jnp.full((EXPERTS * bucket,), row_total, jnp.int32)
    table = table.at[slot.reshape(-1)].set(row_index.reshape(-1), mode='drop')
    padded = jnp.concatenate([normed, jnp.zeros((1, D), jnp.bfloat16)], axis=0)

    def run_expert(expert):
        picks = lax.dynamic_slice(table, (expert * bucket,), (bucket,))
        inputs = padded[picks]
        gate_part = jnp.dot(inputs, gate_w[expert], preferred_element_type=jnp.float32)
        up_part = jnp.dot(inputs, up_w[expert], preferred_element_type=jnp.float32)
        hidden = (jax.nn.silu(gate_part) * up_part).astype(jnp.bfloat16)
        return jnp.dot(hidden, down_w[expert], preferred_element_type=jnp.float32).astype(jnp.bfloat16)
    outputs = lax.map(run_expert, expert_range).reshape(EXPERTS * bucket, D)
    picked = outputs[jnp.minimum(slot, EXPERTS * bucket - 1)]
    shares = (route_scores / lax.optimization_barrier(jnp.sum(route_scores, axis=1, keepdims=True))).astype(jnp.bfloat16)
    mixed = jnp.einsum('rk,rkd->rd', shares.astype(jnp.float32), picked.astype(jnp.float32))
    result = jnp.where(live[:, None], middle_wide + mixed, residual.astype(jnp.float32))
    return result.astype(jnp.bfloat16)
```

```python
import math

import jax
import jax.numpy as jnp
from jax import lax
from jax.experimental import pallas as pl
from jax.experimental.pallas import tpu as pltpu
from jax.sharding import PartitionSpec as P

D = 5120
CAP = 2


def hidden_block(arrivals, gate_w, up_w):
    gate_part = jnp.einsum("secd,edf->secf", arrivals, gate_w, preferred_element_type=jnp.float32)
    up_part = jnp.einsum("secd,edf->secf", arrivals, up_w, preferred_element_type=jnp.float32)
    return (jax.nn.silu(gate_part) * up_part).astype(jnp.bfloat16)


def per_device(
    residual,
    queries,
    cache_keys,
    cache_values,
    new_keys,
    new_values,
    cache_lengths,
    out_proj,
    norm_gain,
    skip_flags,
    expert_ids,
    route_scores,
    gate_w,
    up_w,
    down_w,
):
    rep_count = lax.axis_size("rep")
    local_rows = residual.shape[0]
    column_block = residual.shape[1]
    kv_local = cache_keys.shape[1]
    head_local = queries.shape[1]
    head_size = queries.shape[2]
    scaling = 1.0 / math.sqrt(head_size)
    grouped = queries.reshape(local_rows, kv_local, head_local // kv_local, head_size)
    scores = (
        jnp.einsum("rkgd,rkpd->rkgp", grouped, cache_keys, preferred_element_type=jnp.float32)
        * scaling
    )
    own_score = (
        jnp.einsum("rkgd,rkd->rkg", grouped, new_keys, preferred_element_type=jnp.float32) * scaling
    )
    filled = jnp.arange(cache_keys.shape[2], dtype=jnp.int32)[None, :] < cache_lengths[:, None]
    scores = jnp.where(filled[:, None, None, :], scores, -jnp.inf)
    highest = jnp.maximum(jnp.max(scores, axis=-1), own_score)
    powers = jnp.exp(scores - highest[..., None])
    own_power = jnp.exp(own_score - highest)
    denominator = jnp.sum(powers, axis=-1) + own_power
    probs = (powers / denominator[..., None]).astype(jnp.bfloat16)
    own_prob = (own_power / denominator).astype(jnp.bfloat16)
    attended = jnp.einsum(
        "rkgp,rkpd->rkgd", probs, cache_values, preferred_element_type=jnp.float32
    )
    attended = (
        attended
        + own_prob.astype(jnp.float32)[..., None] * new_values.astype(jnp.float32)[:, :, None, :]
    )
    attended = attended.astype(jnp.bfloat16).reshape(local_rows, head_local * head_size)
    partial_cols = jnp.dot(
        lax.all_gather(attended, "rep", axis=0, tiled=True),
        out_proj,
        preferred_element_type=jnp.float32,
    )
    regrouped = lax.all_to_all(
        partial_cols.astype(jnp.bfloat16), "rep", split_axis=0, concat_axis=1, tiled=True
    ).astype(partial_cols.dtype)
    projected = lax.psum_scatter(
        regrouped.astype(jnp.bfloat16), "head", scatter_dimension=1, tiled=True
    ).astype(jnp.float32)
    middle = (residual.astype(jnp.float32) + projected).astype(jnp.bfloat16)
    middle_wide = middle.astype(jnp.float32)
    exp_local = gate_w.shape[0]
    experts_all = rep_count * exp_local
    slot_count = experts_all * CAP
    top_count = expert_ids.shape[1]
    live = skip_flags == 0
    choose = (
        (expert_ids[:, :, None] == jnp.arange(experts_all, dtype=jnp.int32)[None, None, :])
        & live[:, None, None]
    ).astype(jnp.int32)
    flat_hits = choose.reshape(local_rows * top_count, experts_all)
    before = jnp.cumsum(flat_hits, axis=0) - flat_hits
    rank = jnp.sum(before * flat_hits, axis=1).reshape(local_rows, top_count)
    target = jnp.where(live[:, None], expert_ids * CAP + rank, -1)
    marks = (target[:, :, None] == jnp.arange(slot_count, dtype=jnp.int32)[None, None, :]).astype(
        jnp.float32
    )
    placing = jnp.sum(marks, axis=1).astype(jnp.bfloat16)
    shares = (route_scores / jnp.sum(route_scores, axis=1, keepdims=True)).astype(jnp.bfloat16)
    combine = jnp.sum(marks * shares.astype(jnp.float32)[:, :, None], axis=1).astype(jnp.bfloat16)
    full_middle = lax.all_gather(middle, "head", axis=1, tiled=True).astype(jnp.float32)
    mean_square = jnp.mean(full_middle * full_middle, axis=-1, keepdims=True)
    normed = (full_middle * lax.rsqrt(mean_square + 1e-05) * norm_gain[None, :]).astype(
        jnp.bfloat16
    )
    outgoing = jnp.einsum("rs,rd->sd", placing, normed, preferred_element_type=jnp.float32).astype(
        jnp.bfloat16
    )
    outgoing = outgoing.reshape(rep_count, exp_local, CAP, D)
    hidden = hidden_block(
        lax.all_to_all(outgoing, "rep", split_axis=0, concat_axis=0, tiled=True), gate_w, up_w
    )
    partial_out = jnp.einsum("secf,efd->secd", hidden, down_w, preferred_element_type=jnp.float32)
    summed = lax.psum_scatter(
        partial_out.astype(jnp.bfloat16), "head", scatter_dimension=3, tiled=True
    )
    expert_out = lax.all_to_all(summed, "rep", split_axis=0, concat_axis=0, tiled=True)
    expert_out = expert_out.reshape(slot_count, column_block)
    mixed = jnp.dot(combine, expert_out, preferred_element_type=jnp.float32)
    result = jnp.where(live[:, None], middle_wide + mixed, residual.astype(jnp.float32))
    return result.astype(jnp.bfloat16)


MESH = pl.DeviceIdType.MESH
N = 4
ROWS = 4
ALL = N * ROWS
HEAD_SIZE = 128
PIECE = 384
STARTS = (0, 384, 768, 1024)
WIDTHS = (384, 384, 256, 256)


def fits_fused(mesh):
    return mesh.shape["rep"] == N and mesh.shape["head"] == N


def pack_rows(x):
    pieces = []
    for start, width in zip(STARTS, WIDTHS):
        piece = x[:, start : start + width]
        if width < PIECE:
            piece = jnp.concatenate(
                [piece, jnp.zeros((x.shape[0], PIECE - width), x.dtype)], axis=1
            )
        pieces.append(piece)
    return jnp.concatenate(pieces, axis=0)


def unpack_rows(y):
    return jnp.concatenate(
        [y[ROWS * i : ROWS * (i + 1), :width] for i, width in enumerate(WIDTHS)], axis=1
    )


def by_row(shape, group, read):
    row = lax.broadcasted_iota(jnp.int32, shape, 0) // group
    out = jnp.full(shape, read(0))
    for i in range(1, shape[0] // group):
        out = jnp.where(row == i, read(i), out)
    return out


def dot(a, b):
    return jnp.dot(a, b, preferred_element_type=jnp.float32)


def fused_kernel(
    queries,
    cache_keys,
    cache_values,
    new_keys,
    new_values,
    residual,
    out_proj,
    norm_gain,
    gate_w,
    up_w,
    down_w,
    lengths,
    skips,
    ids,
    routes,
    out,
    q_v,
    k_v,
    v_v,
    nk_v,
    nv_v,
    res_v,
    w_v,
    gain_v,
    gate_v,
    up_v,
    down_v,
    att_f,
    att_all,
    att_wide,
    res_pack,
    res_in,
    proj_out,
    proj_in,
    mid_all,
    exp_out,
    exp_in,
    back_out,
    back_in,
    load_sem,
    w_sem,
    att_send,
    att_recv,
    res_send,
    res_recv,
    proj_send,
    proj_recv,
    mid_send,
    fwd_send,
    mid_recv,
    exp_send,
    exp_recv,
    back_send,
    back_recv,
):
    g = lax.axis_index("groups")
    r = lax.axis_index("rep")
    h = lax.axis_index("head")

    def remote(src, dst, send, recv, to_rep, to_head):
        return pltpu.make_async_remote_copy(
            src_ref=src,
            dst_ref=dst,
            send_sem=send,
            recv_sem=recv,
            device_id=(g, to_rep, to_head),
            device_id_type=MESH,
        )

    barrier = pltpu.get_barrier_semaphore()
    for i in range(N):
        for j in range(N):

            @pl.when(jnp.logical_or(r != i, h != j))
            def _():
                pl.semaphore_signal(barrier, inc=1, device_id=(g, i, j), device_id_type=MESH)

    loads = [
        pltpu.make_async_copy(src, dst, load_sem.at[i])
        for i, (src, dst) in enumerate(
            (
                (queries, q_v),
                (cache_keys, k_v),
                (new_keys, nk_v),
                (new_values, nv_v),
                (residual, res_v),
                (cache_values, v_v),
                (norm_gain, gain_v),
                (gate_w, gate_v),
                (up_w, up_v),
                (down_w, down_v),
            )
        )
    ]
    depth = w_v.shape[0] // N
    w_loads = [
        pltpu.make_async_copy(
            out_proj.at[pl.ds(c * depth, depth)], w_v.at[pl.ds(c * depth, depth)], w_sem.at[c]
        )
        for c in range(N)
    ]
    for copy in loads[:6]:
        copy.start()
    for copy in w_loads:
        copy.start()
    for copy in loads[6:]:
        copy.start()

    heads = q_v.shape[1]
    kv = k_v.shape[1]
    lines = ROWS * heads
    blocks = ROWS * kv
    per_block = heads // kv
    scaling = 1.0 / math.sqrt(HEAD_SIZE)
    loads[0].wait()
    q = q_v[...].astype(jnp.float32).reshape(lines, HEAD_SIZE).astype(jnp.bfloat16)
    loads[1].wait()
    keys = k_v[...].reshape(blocks * k_v.shape[2], HEAD_SIZE)
    slots = k_v.shape[2]
    wide = lax.dot_general(
        q, keys, (((1,), (1,)), ((), ())), preferred_element_type=jnp.float32
    )
    block = lax.broadcasted_iota(jnp.int32, (lines, slots), 0) // per_block
    scores = wide[:, :slots]
    for t in range(1, blocks):
        scores = jnp.where(block == t, wide[:, t * slots : (t + 1) * slots], scores)
    scores = scores * scaling
    loads[2].wait()
    loads[3].wait()
    nk = jnp.concatenate([nk_v[i].astype(jnp.float32) for i in range(ROWS)], axis=0)
    nv = jnp.concatenate([nv_v[i].astype(jnp.float32) for i in range(ROWS)], axis=0)
    own_wide = lax.dot_general(
        q, nk.astype(jnp.bfloat16), (((1,), (1,)), ((), ())), preferred_element_type=jnp.float32
    )
    own_here = lax.broadcasted_iota(
        jnp.int32, (lines, blocks), 0
    ) // per_block == lax.broadcasted_iota(jnp.int32, (lines, blocks), 1)
    own = jnp.sum(jnp.where(own_here, own_wide, 0.0), axis=1, keepdims=True) * scaling
    filled = lax.broadcasted_iota(jnp.int32, (lines, slots), 1) < by_row(
        (lines, slots), heads, lambda i: lengths[i]
    )
    scores = jnp.where(filled, scores, -jnp.inf)
    highest = jnp.maximum(jnp.max(scores, axis=1, keepdims=True), own)
    powers = jnp.exp(scores - highest)
    own_power = jnp.exp(own - highest)
    denominator = jnp.sum(powers, axis=1, keepdims=True) + own_power
    probs = powers / denominator
    own_prob = own_power / denominator
    spread = jnp.concatenate(
        [jnp.where(block == t, probs, 0.0).astype(jnp.bfloat16) for t in range(blocks)], axis=1
    )
    own_spread = jnp.where(own_here, own_prob, 0.0).astype(jnp.bfloat16)
    loads[5].wait()
    att = dot(spread, v_v[...].reshape(blocks * slots, HEAD_SIZE))
    att_f[...] = att + dot(own_spread, nv.astype(jnp.bfloat16))
    per_quarter = heads // N
    att_all[r] = jnp.concatenate(
        [att_f[pl.ds(j, ALL, stride=per_quarter), :] for j in range(per_quarter)], axis=1
    ).astype(jnp.bfloat16)
    loads[4].wait()
    res = res_v[...].astype(jnp.float32)
    res_pack[...] = pack_rows(res).astype(jnp.bfloat16)

    pl.semaphore_wait(barrier, N * N - 1)

    def att_copy(i):
        return remote(att_all.at[r], att_all.at[r], att_send.at[i], att_recv.at[r], i, h)

    def att_arrival(i):
        return remote(att_all.at[i], att_all.at[i], att_send.at[i], att_recv.at[i], i, h)

    def res_copy(j):
        return remote(res_pack, res_in.at[r], res_send.at[j], res_recv.at[r], h, j)

    def res_arrival(i):
        return remote(res_pack, res_in.at[i], res_send.at[i], res_recv.at[i], i, r)

    for i in range(N):

        @pl.when(r != i)
        def _():
            att_copy(i).start()

    for j in range(N):

        @pl.when(jnp.logical_or(r != h, h != j))
        def _():
            res_copy(j).start()

    @pl.when(r == h)
    def _():
        res_in[r] = res_pack[...]

    for i in range(N):

        @pl.when(r != i)
        def _():
            att_arrival(i).wait_recv()

    for t in range(per_quarter):
        cut = att_all[:, :, t * HEAD_SIZE : (t + 1) * HEAD_SIZE]
        att_wide[t] = cut.astype(jnp.float32).reshape(N * ALL, HEAD_SIZE)
    total = None
    for c in range(N):
        w_loads[c].wait()
        lhs = jnp.concatenate(
            [att_wide[t, pl.ds(c, ALL, stride=N), :] for t in range(per_quarter)], axis=1
        ).astype(jnp.bfloat16)
        part = dot(lhs, w_v[pl.ds(c * depth, depth), :])
        total = part if total is None else total + part

    def proj_copy(j):
        return remote(proj_out.at[j], proj_in.at[h], proj_send.at[j], proj_recv.at[h], r, j)

    def proj_arrival(j):
        return remote(proj_out.at[j], proj_in.at[j], proj_send.at[j], proj_recv.at[j], r, j)

    for j in range(N):
        piece = total[:, STARTS[j] : STARTS[j] + WIDTHS[j]].astype(jnp.bfloat16)
        proj_out[j, :, : WIDTHS[j]] = piece
        if WIDTHS[j] < PIECE:
            proj_out[j, :, WIDTHS[j] :] = jnp.zeros((ALL, PIECE - WIDTHS[j]), jnp.bfloat16)

        @pl.when(h != j)
        def _():
            proj_copy(j).start()

        @pl.when(h == j)
        def _():
            proj_in[j] = proj_out[j]

    for i in range(N):

        @pl.when(jnp.logical_or(r != h, r != i))
        def _():
            res_arrival(i).wait_recv()

    res_all = [res_in[i].astype(jnp.float32) for i in range(N)]
    middle = jnp.zeros((ALL, PIECE), jnp.float32)
    for j in range(N):
        mine = jnp.concatenate([x[ROWS * j : ROWS * (j + 1)] for x in res_all], axis=0)
        middle = jnp.where(h == j, mine, middle)
    for j in range(N):

        @pl.when(h != j)
        def _():
            proj_arrival(j).wait_recv()

    summed = proj_in[0].astype(jnp.float32)
    for j in range(1, N):
        summed = summed + proj_in[j].astype(jnp.float32)
    mid_all[r, h] = (middle + summed).astype(jnp.bfloat16)

    def mid_copy(i):
        return remote(
            mid_all.at[r, h], mid_all.at[r, h], mid_send.at[i], mid_recv.at[r, h], i, h
        )

    def mid_arrival(i, j):
        return remote(
            mid_all.at[i, j], mid_all.at[i, j], mid_send.at[i], mid_recv.at[i, j], i, j
        )

    def mid_forward(i, j):
        return remote(
            mid_all.at[i, h], mid_all.at[i, h], fwd_send.at[i, j], mid_recv.at[i, h], r, j
        )

    for i in range(N):

        @pl.when(r != i)
        def _():
            mid_copy(i).start()

    for j in range(N):

        @pl.when(h != j)
        def _():
            mid_forward(r, j).start()

    for i in range(N):

        @pl.when(r != i)
        def _():
            mid_arrival(i, h).wait_recv()
            for j in range(N):

                @pl.when(h != j)
                def _():
                    mid_forward(i, j).start()

    for i in range(6, 10):
        loads[i].wait()
    for i in range(N):
        for j in range(N):

            @pl.when(h != j)
            def _():
                mid_arrival(i, j).wait_recv()

    rows = []
    squares = jnp.zeros((ALL, 1), jnp.float32)
    for i in range(N):
        x = jnp.concatenate([mid_all[i, j][:, : WIDTHS[j]] for j in range(N)], axis=1).astype(
            jnp.float32
        )
        rows.append(x)
        squares = squares + jnp.sum(x * x, axis=1, keepdims=True)
    columns = rows[0].shape[1]
    scale = lax.rsqrt(squares * (1.0 / (N * columns)) + 1e-05)
    gate = jnp.zeros((ALL, gate_v.shape[2]), jnp.float32)
    up = jnp.zeros((ALL, up_v.shape[2]), jnp.float32)
    for i in range(N):
        cut = pl.ds(i * columns, columns)
        normed = (rows[i] * scale * gain_v[:, cut]).astype(jnp.bfloat16)
        gate = gate + dot(normed, gate_v[0, cut, :])
        up = up + dot(normed, up_v[0, cut, :])
    hidden = (gate / (1.0 + jnp.exp(-gate)) * up).astype(jnp.bfloat16)

    def exp_copy(j):
        return remote(exp_out.at[j], exp_in.at[h], exp_send.at[j], exp_recv.at[h], r, j)

    def exp_arrival(j):
        return remote(exp_out.at[j], exp_in.at[j], exp_send.at[j], exp_recv.at[j], r, j)

    for j in range(N):
        exp_out[j] = dot(hidden, down_v[0, :, pl.ds(j * columns, columns)]).astype(jnp.bfloat16)

        @pl.when(h != j)
        def _():
            exp_copy(j).start()

        @pl.when(h == j)
        def _():
            exp_in[j] = exp_out[j]

    line = lax.broadcasted_iota(jnp.int32, (ROWS, ALL), 1)
    want = lax.broadcasted_iota(jnp.int32, (ROWS, ALL), 0) + r * ROWS
    pick = jnp.where(line == want, 1.0, 0.0).astype(jnp.bfloat16)
    mine = jnp.concatenate([mid_all[h, j][:, : WIDTHS[j]] for j in range(N)], axis=1)
    own_mid = dot(pick, mine)
    top = ids.shape[0]
    packed = (ALL, PIECE)
    place = lax.broadcasted_iota(jnp.int32, packed, 0) % ROWS

    def spread_rows(read):
        result = jnp.full(packed, read(0))
        for i in range(1, ROWS):
            result = jnp.where(place == i, read(i), result)
        return result

    scored = [spread_rows(lambda i, k=k: routes[k, i]) for k in range(top)]
    named = [spread_rows(lambda i, k=k: ids[k, i]) for k in range(top)]
    whole = sum(scored[1:], scored[0])
    shares = [(s / whole).astype(jnp.bfloat16).astype(jnp.float32) for s in scored]
    weights = [
        sum(jnp.where(named[k] == e, shares[k], 0.0) for k in range(top)) for e in range(N)
    ]

    for j in range(N):

        @pl.when(h != j)
        def _():
            exp_arrival(j).wait_recv()

    expert = exp_in[0].astype(jnp.float32)
    for j in range(1, N):
        expert = expert + exp_in[j].astype(jnp.float32)

    def back_copy(i):
        return remote(back_out.at[i], back_in.at[r], back_send.at[i], back_recv.at[r], i, h)

    def back_arrival(i):
        return remote(back_out.at[i], back_in.at[i], back_send.at[i], back_recv.at[i], i, h)

    for i in range(N):
        back_out[i] = pack_rows(expert[ROWS * i : ROWS * (i + 1)]).astype(jnp.bfloat16)

        @pl.when(r != i)
        def _():
            back_copy(i).start()

        @pl.when(r == i)
        def _():
            back_in[i] = back_out[i]

    for i in range(N):

        @pl.when(r != i)
        def _():
            back_arrival(i).wait_recv()

    mixed = weights[0] * back_in[0].astype(jnp.float32)
    for e in range(1, N):
        mixed = mixed + weights[e] * back_in[e].astype(jnp.float32)
    skipped = by_row((ROWS, columns), 1, lambda i: skips[i])
    out[...] = jnp.where(skipped == 0, own_mid + unpack_rows(mixed), res).astype(jnp.bfloat16)

    for i in range(N):

        @pl.when(r != i)
        def _():
            att_copy(i).wait_send()
            mid_copy(i).wait_send()
            back_copy(i).wait_send()

        @pl.when(h != i)
        def _():
            proj_copy(i).wait_send()
            exp_copy(i).wait_send()
            for k in range(N):
                mid_forward(k, i).wait_send()

        @pl.when(jnp.logical_or(r != h, h != i))
        def _():
            res_copy(i).wait_send()


def fused_device(
    residual,
    queries,
    cache_keys,
    cache_values,
    new_keys,
    new_values,
    cache_lengths,
    out_proj,
    norm_gain,
    skip_flags,
    expert_ids,
    route_scores,
    gate_w,
    up_w,
    down_w,
):
    bf16, f32 = jnp.bfloat16, jnp.float32
    gain = norm_gain[None, :]
    inputs = (
        queries,
        cache_keys,
        cache_values,
        new_keys,
        new_values,
        residual,
        out_proj,
        gain,
        gate_w,
        up_w,
        down_w,
    )
    heads = queries.shape[1]
    columns = residual.shape[1]
    depth = heads * HEAD_SIZE // N
    dma = pltpu.SemaphoreType.DMA
    return pl.pallas_call(
        fused_kernel,
        out_shape=jax.ShapeDtypeStruct(residual.shape, bf16),
        in_specs=[pl.BlockSpec(memory_space=pl.ANY)] * len(inputs)
        + [pl.BlockSpec(memory_space=pltpu.SMEM)] * 4,
        out_specs=pl.BlockSpec(memory_space=pltpu.VMEM),
        scratch_shapes=[pltpu.VMEM(x.shape, x.dtype) for x in inputs]
        + [
            pltpu.VMEM((ROWS * heads, HEAD_SIZE), f32),
            pltpu.VMEM((N, ALL, depth), bf16),
            pltpu.VMEM((depth // HEAD_SIZE, N * ALL, HEAD_SIZE), f32),
            pltpu.VMEM((ALL, PIECE), bf16),
            pltpu.VMEM((N, ALL, PIECE), bf16),
            pltpu.VMEM((N, ALL, PIECE), bf16),
            pltpu.VMEM((N, ALL, PIECE), bf16),
            pltpu.VMEM((N, N, ALL, PIECE), bf16),
            pltpu.VMEM((N, ALL, columns), bf16),
            pltpu.VMEM((N, ALL, columns), bf16),
            pltpu.VMEM((N, ALL, PIECE), bf16),
            pltpu.VMEM((N, ALL, PIECE), bf16),
            dma((10,)),
            dma((N,)),
            dma((N,)),
            dma((N,)),
            dma((N,)),
            dma((N,)),
            dma((N,)),
            dma((N,)),
            dma((N,)),
            dma((N, N)),
            dma((N, N)),
            dma((N,)),
            dma((N,)),
            dma((N,)),
            dma((N,)),
        ],
        compiler_params=pltpu.CompilerParams(
            collective_id=0, has_side_effects=True, vmem_limit_bytes=63 * 1024 * 1024
        ),
    )(*inputs, cache_lengths, skip_flags, expert_ids.T, route_scores.T)


def solution(mesh):
    return jax.shard_map(
        fused_device if fits_fused(mesh) else per_device,
        mesh=mesh,
        in_specs=(
            P(("groups", "rep"), "head"),
            P(("groups", "rep"), "head", None),
            P(("groups", "rep"), "head", None, None),
            P(("groups", "rep"), "head", None, None),
            P(("groups", "rep"), "head", None),
            P(("groups", "rep"), "head", None),
            P(("groups", "rep")),
            P("head", "rep"),
            P(),
            P(("groups", "rep")),
            P(("groups", "rep"), None),
            P(("groups", "rep"), None),
            P("rep", None, "head"),
            P("rep", None, "head"),
            P("rep", "head", None),
        ),
        out_specs=P(("groups", "rep"), "head"),
        check_vma=False,
    )
```

```python
import math

import jax
import jax.numpy as jnp
from jax import lax
from jax.experimental import pallas as pl
from jax.experimental.pallas import tpu as pltpu
from jax.sharding import PartitionSpec as P

D = 5120
CAP = 2


def hidden_block(arrivals, gate_w, up_w):
    gate_part = jnp.einsum("secd,edf->secf", arrivals, gate_w, preferred_element_type=jnp.float32)
    up_part = jnp.einsum("secd,edf->secf", arrivals, up_w, preferred_element_type=jnp.float32)
    return (jax.nn.silu(gate_part) * up_part).astype(jnp.bfloat16)


def per_device(
    residual,
    queries,
    cache_keys,
    cache_values,
    new_keys,
    new_values,
    cache_lengths,
    out_proj,
    norm_gain,
    skip_flags,
    expert_ids,
    route_scores,
    gate_w,
    up_w,
    down_w,
):
    rep_count = lax.axis_size("rep")
    local_rows = residual.shape[0]
    column_block = residual.shape[1]
    kv_local = cache_keys.shape[1]
    head_local = queries.shape[1]
    head_size = queries.shape[2]
    scaling = 1.0 / math.sqrt(head_size)
    grouped = queries.reshape(local_rows, kv_local, head_local // kv_local, head_size)
    scores = (
        jnp.einsum("rkgd,rkpd->rkgp", grouped, cache_keys, preferred_element_type=jnp.float32)
        * scaling
    )
    own_score = (
        jnp.einsum("rkgd,rkd->rkg", grouped, new_keys, preferred_element_type=jnp.float32) * scaling
    )
    filled = jnp.arange(cache_keys.shape[2], dtype=jnp.int32)[None, :] < cache_lengths[:, None]
    scores = jnp.where(filled[:, None, None, :], scores, -jnp.inf)
    highest = jnp.maximum(jnp.max(scores, axis=-1), own_score)
    powers = jnp.exp(scores - highest[..., None])
    own_power = jnp.exp(own_score - highest)
    denominator = jnp.sum(powers, axis=-1) + own_power
    probs = (powers / denominator[..., None]).astype(jnp.bfloat16)
    own_prob = (own_power / denominator).astype(jnp.bfloat16)
    attended = jnp.einsum(
        "rkgp,rkpd->rkgd", probs, cache_values, preferred_element_type=jnp.float32
    )
    attended = (
        attended
        + own_prob.astype(jnp.float32)[..., None] * new_values.astype(jnp.float32)[:, :, None, :]
    )
    attended = attended.astype(jnp.bfloat16).reshape(local_rows, head_local * head_size)
    partial_cols = jnp.dot(
        lax.all_gather(attended, "rep", axis=0, tiled=True),
        out_proj,
        preferred_element_type=jnp.float32,
    )
    regrouped = lax.all_to_all(
        partial_cols.astype(jnp.bfloat16), "rep", split_axis=0, concat_axis=1, tiled=True
    ).astype(partial_cols.dtype)
    projected = lax.psum_scatter(
        regrouped.astype(jnp.bfloat16), "head", scatter_dimension=1, tiled=True
    ).astype(jnp.float32)
    middle = (residual.astype(jnp.float32) + projected).astype(jnp.bfloat16)
    middle_wide = middle.astype(jnp.float32)
    exp_local = gate_w.shape[0]
    experts_all = rep_count * exp_local
    slot_count = experts_all * CAP
    top_count = expert_ids.shape[1]
    live = skip_flags == 0
    choose = (
        (expert_ids[:, :, None] == jnp.arange(experts_all, dtype=jnp.int32)[None, None, :])
        & live[:, None, None]
    ).astype(jnp.int32)
    flat_hits = choose.reshape(local_rows * top_count, experts_all)
    before = jnp.cumsum(flat_hits, axis=0) - flat_hits
    rank = jnp.sum(before * flat_hits, axis=1).reshape(local_rows, top_count)
    target = jnp.where(live[:, None], expert_ids * CAP + rank, -1)
    marks = (target[:, :, None] == jnp.arange(slot_count, dtype=jnp.int32)[None, None, :]).astype(
        jnp.float32
    )
    placing = jnp.sum(marks, axis=1).astype(jnp.bfloat16)
    shares = (route_scores / jnp.sum(route_scores, axis=1, keepdims=True)).astype(jnp.bfloat16)
    combine = jnp.sum(marks * shares.astype(jnp.float32)[:, :, None], axis=1).astype(jnp.bfloat16)
    full_middle = lax.all_gather(middle, "head", axis=1, tiled=True).astype(jnp.float32)
    mean_square = jnp.mean(full_middle * full_middle, axis=-1, keepdims=True)
    normed = (full_middle * lax.rsqrt(mean_square + 1e-05) * norm_gain[None, :]).astype(
        jnp.bfloat16
    )
    outgoing = jnp.einsum("rs,rd->sd", placing, normed, preferred_element_type=jnp.float32).astype(
        jnp.bfloat16
    )
    outgoing = outgoing.reshape(rep_count, exp_local, CAP, D)
    hidden = hidden_block(
        lax.all_to_all(outgoing, "rep", split_axis=0, concat_axis=0, tiled=True), gate_w, up_w
    )
    partial_out = jnp.einsum("secf,efd->secd", hidden, down_w, preferred_element_type=jnp.float32)
    summed = lax.psum_scatter(
        partial_out.astype(jnp.bfloat16), "head", scatter_dimension=3, tiled=True
    )
    expert_out = lax.all_to_all(summed, "rep", split_axis=0, concat_axis=0, tiled=True)
    expert_out = expert_out.reshape(slot_count, column_block)
    mixed = jnp.dot(combine, expert_out, preferred_element_type=jnp.float32)
    result = jnp.where(live[:, None], middle_wide + mixed, residual.astype(jnp.float32))
    return result.astype(jnp.bfloat16)


MESH = pl.DeviceIdType.MESH
N = 4
ROWS = 4
ALL = N * ROWS
HEAD_SIZE = 128
PIECE = 384
STARTS = (0, 384, 768, 1024)
WIDTHS = (384, 384, 256, 256)


def fits_fused(mesh):
    return mesh.shape["rep"] == N and mesh.shape["head"] == N


def pack_rows(x):
    pieces = []
    for start, width in zip(STARTS, WIDTHS):
        piece = x[:, start : start + width]
        if width < PIECE:
            piece = jnp.concatenate(
                [piece, jnp.zeros((x.shape[0], PIECE - width), x.dtype)], axis=1
            )
        pieces.append(piece)
    return jnp.concatenate(pieces, axis=0)


def unpack_rows(y):
    return jnp.concatenate(
        [y[ROWS * i : ROWS * (i + 1), :width] for i, width in enumerate(WIDTHS)], axis=1
    )


def by_row(shape, group, read):
    row = lax.broadcasted_iota(jnp.int32, shape, 0) // group
    out = jnp.full(shape, read(0))
    for i in range(1, shape[0] // group):
        out = jnp.where(row == i, read(i), out)
    return out


def dot(a, b):
    return jnp.dot(a, b, preferred_element_type=jnp.float32)


def fused_kernel(
    queries,
    cache_keys,
    cache_values,
    new_keys,
    new_values,
    residual,
    out_proj,
    norm_gain,
    gate_w,
    up_w,
    down_w,
    cache_lengths,
    skip_flags,
    expert_ids,
    route_scores,
    out,
    q_v,
    k_v,
    v_v,
    nk_v,
    nv_v,
    res_v,
    w_v,
    gain_v,
    gate_v,
    up_v,
    down_v,
    lengths,
    skips,
    ids,
    routes,
    att_f,
    att_all,
    att_wide,
    res_pack,
    res_in,
    proj_out,
    proj_in,
    mid_all,
    exp_out,
    exp_in,
    back_out,
    back_in,
    load_sem,
    w_sem,
    att_send,
    att_recv,
    res_send,
    res_recv,
    proj_send,
    proj_recv,
    mid_send,
    across_send,
    beside_send,
    mid_recv,
    exp_send,
    exp_recv,
    back_send,
    back_recv,
):
    g = lax.axis_index("groups")
    r = lax.axis_index("rep")
    h = lax.axis_index("head")

    def remote(src, dst, send, recv, to_rep, to_head):
        return pltpu.make_async_remote_copy(
            src_ref=src,
            dst_ref=dst,
            send_sem=send,
            recv_sem=recv,
            device_id=(g, to_rep, to_head),
            device_id_type=MESH,
        )

    across = lax.rem(h + 2, N)
    beside = h + 1 - 2 * lax.rem(h, 2)
    barrier = pltpu.get_barrier_semaphore()
    for i in range(N):

        @pl.when(r != i)
        def _():
            pl.semaphore_signal(barrier, inc=1, device_id=(g, i, h), device_id_type=MESH)

        @pl.when(h != i)
        def _():
            pl.semaphore_signal(barrier, inc=1, device_id=(g, r, i), device_id_type=MESH)

    loads = [
        pltpu.make_async_copy(src, dst, load_sem.at[i])
        for i, (src, dst) in enumerate(
            (
                (queries, q_v),
                (cache_keys, k_v),
                (new_keys, nk_v),
                (new_values, nv_v),
                (residual, res_v),
                (cache_values, v_v),
                (norm_gain, gain_v),
                (gate_w, gate_v),
                (up_w, up_v),
                (down_w, down_v),
                (cache_lengths, lengths),
                (skip_flags, skips),
                (expert_ids, ids),
                (route_scores, routes),
            )
        )
    ]
    depth = w_v.shape[0] // N
    w_loads = [
        pltpu.make_async_copy(
            out_proj.at[pl.ds(c * depth, depth)], w_v.at[pl.ds(c * depth, depth)], w_sem.at[c]
        )
        for c in range(N)
    ]
    for copy in loads[10:] + loads[:6] + w_loads + loads[6:10]:
        copy.start()

    heads = q_v.shape[1]
    kv = k_v.shape[1]
    lines = ROWS * heads
    blocks = ROWS * kv
    per_block = heads // kv
    scaling = 1.0 / math.sqrt(HEAD_SIZE)
    loads[0].wait()
    q = q_v[...].astype(jnp.float32).reshape(lines, HEAD_SIZE).astype(jnp.bfloat16)
    loads[1].wait()
    keys = k_v[...].reshape(blocks * k_v.shape[2], HEAD_SIZE)
    slots = k_v.shape[2]
    wide = lax.dot_general(
        q, keys, (((1,), (1,)), ((), ())), preferred_element_type=jnp.float32
    )
    block = lax.broadcasted_iota(jnp.int32, (lines, slots), 0) // per_block
    scores = wide[:, :slots]
    for t in range(1, blocks):
        scores = jnp.where(block == t, wide[:, t * slots : (t + 1) * slots], scores)
    scores = scores * scaling
    loads[2].wait()
    loads[3].wait()
    nk = jnp.concatenate([nk_v[i].astype(jnp.float32) for i in range(ROWS)], axis=0)
    nv = jnp.concatenate([nv_v[i].astype(jnp.float32) for i in range(ROWS)], axis=0)
    own_wide = lax.dot_general(
        q, nk.astype(jnp.bfloat16), (((1,), (1,)), ((), ())), preferred_element_type=jnp.float32
    )
    own_here = lax.broadcasted_iota(
        jnp.int32, (lines, blocks), 0
    ) // per_block == lax.broadcasted_iota(jnp.int32, (lines, blocks), 1)
    own = jnp.sum(jnp.where(own_here, own_wide, 0.0), axis=1, keepdims=True) * scaling
    for copy in loads[10:]:
        copy.wait()
    filled = lax.broadcasted_iota(jnp.int32, (lines, slots), 1) < by_row(
        (lines, slots), heads, lambda i: lengths[i]
    )
    scores = jnp.where(filled, scores, -jnp.inf)
    highest = jnp.maximum(jnp.max(scores, axis=1, keepdims=True), own)
    powers = jnp.exp(scores - highest)
    own_power = jnp.exp(own - highest)
    denominator = jnp.sum(powers, axis=1, keepdims=True) + own_power
    probs = powers / denominator
    own_prob = own_power / denominator
    spread = jnp.concatenate(
        [jnp.where(block == t, probs, 0.0).astype(jnp.bfloat16) for t in range(blocks)], axis=1
    )
    own_spread = jnp.where(own_here, own_prob, 0.0).astype(jnp.bfloat16)
    loads[5].wait()
    att = dot(spread, v_v[...].reshape(blocks * slots, HEAD_SIZE))
    att_f[...] = att + dot(own_spread, nv.astype(jnp.bfloat16))
    per_quarter = heads // N
    att_all[r] = jnp.concatenate(
        [att_f[pl.ds(j, ALL, stride=per_quarter), :] for j in range(per_quarter)], axis=1
    ).astype(jnp.bfloat16)
    loads[4].wait()
    res = res_v[...].astype(jnp.float32)
    res_pack[...] = pack_rows(res).astype(jnp.bfloat16)

    pl.semaphore_wait(barrier, 2 * (N - 1))

    def att_copy(i):
        return remote(att_all.at[r], att_all.at[r], att_send.at[i], att_recv.at[r], i, h)

    def att_arrival(i):
        return remote(att_all.at[i], att_all.at[i], att_send.at[i], att_recv.at[i], i, h)

    def res_copy():
        return remote(res_pack, res_in.at[r], res_send, res_recv.at[r], h, h)

    def res_arrival(i):
        return remote(res_pack, res_in.at[i], res_send, res_recv.at[i], i, h)

    for i in range(N):

        @pl.when(r != i)
        def _():
            att_copy(i).start()

    @pl.when(r != h)
    def _():
        res_copy().start()

    @pl.when(r == h)
    def _():
        res_in[r] = res_pack[...]

    for i in range(N):

        @pl.when(r != i)
        def _():
            att_arrival(i).wait_recv()

    for t in range(per_quarter):
        cut = att_all[:, :, t * HEAD_SIZE : (t + 1) * HEAD_SIZE]
        att_wide[t] = cut.astype(jnp.float32).reshape(N * ALL, HEAD_SIZE)
    @pl.when(r == h)
    def _():
        for i in range(N):

            @pl.when(r != i)
            def _():
                res_arrival(i).wait_recv()

    @pl.when(r != h)
    def _():
        res_in[...] = jnp.zeros_like(res_in)

    total = jnp.concatenate(
        [unpack_rows(res_in[i].astype(jnp.float32)) for i in range(N)], axis=0
    )
    for c in range(N):
        w_loads[c].wait()
        lhs = jnp.concatenate(
            [att_wide[t, pl.ds(c, ALL, stride=N), :] for t in range(per_quarter)], axis=1
        ).astype(jnp.bfloat16)
        part = dot(lhs, w_v[pl.ds(c * depth, depth), :])
        total = total + part

    def proj_copy(j):
        return remote(proj_out.at[j], proj_in.at[h], proj_send.at[j], proj_recv.at[h], r, j)

    def proj_arrival(j):
        return remote(proj_out.at[j], proj_in.at[j], proj_send.at[j], proj_recv.at[j], r, j)

    for j in range(N):
        piece = total[:, STARTS[j] : STARTS[j] + WIDTHS[j]].astype(jnp.bfloat16)
        proj_out[j, :, : WIDTHS[j]] = piece
        if WIDTHS[j] < PIECE:
            proj_out[j, :, WIDTHS[j] :] = jnp.zeros((ALL, PIECE - WIDTHS[j]), jnp.bfloat16)

        @pl.when(h != j)
        def _():
            proj_copy(j).start()

        @pl.when(h == j)
        def _():
            proj_in[j] = proj_out[j]

    for j in range(N):

        @pl.when(h != j)
        def _():
            proj_arrival(j).wait_recv()

    summed = proj_in[0].astype(jnp.float32)
    for j in range(1, N):
        summed = summed + proj_in[j].astype(jnp.float32)
    mid_all[r, h] = summed.astype(jnp.bfloat16)

    def mid_copy(i):
        return remote(
            mid_all.at[r, h], mid_all.at[r, h], mid_send.at[i], mid_recv.at[r, h], i, h
        )

    def mid_arrival(i, j):
        return remote(
            mid_all.at[i, j], mid_all.at[i, j], mid_send.at[0], mid_recv.at[i, j], r, beside
        )

    def mid_across(i):
        return remote(
            mid_all.at[i, h], mid_all.at[i, h], across_send.at[i], mid_recv.at[i, h], r, across
        )

    def mid_beside(i, k):
        j = (h, across)[k]
        return remote(
            mid_all.at[i, j],
            mid_all.at[i, j],
            beside_send.at[i, k],
            mid_recv.at[i, j],
            r,
            beside,
        )

    for i in range(N):

        @pl.when(r != i)
        def _():
            mid_copy(i).start()

    mid_across(r).start()
    mid_beside(r, 0).start()
    for turn in range(1, N):
        i = lax.rem(r + turn, N)
        mid_arrival(i, h).wait_recv()
        mid_across(i).start()
        mid_beside(i, 0).start()
    for turn in range(N):
        i = lax.rem(r + turn, N)
        mid_arrival(i, across).wait_recv()
        mid_beside(i, 1).start()
    for i in range(6, 10):
        loads[i].wait()
    far = lax.rem(beside + 2, N)
    for i in range(N):
        mid_arrival(i, beside).wait_recv()
        mid_arrival(i, far).wait_recv()

    rows = []
    squares = jnp.zeros((ALL, 1), jnp.float32)
    for i in range(N):
        x = jnp.concatenate([mid_all[i, j][:, : WIDTHS[j]] for j in range(N)], axis=1).astype(
            jnp.float32
        )
        rows.append(x)
        squares = squares + jnp.sum(x * x, axis=1, keepdims=True)
    columns = rows[0].shape[1]
    scale = lax.rsqrt(squares * (1.0 / (N * columns)) + 1e-05)
    gate = jnp.zeros((ALL, gate_v.shape[2]), jnp.float32)
    up = jnp.zeros((ALL, up_v.shape[2]), jnp.float32)
    for i in range(N):
        cut = pl.ds(i * columns, columns)
        normed = (rows[i] * scale * gain_v[:, cut]).astype(jnp.bfloat16)
        gate = gate + dot(normed, gate_v[0, cut, :])
        up = up + dot(normed, up_v[0, cut, :])
    hidden = (gate / (1.0 + jnp.exp(-gate)) * up).astype(jnp.bfloat16)

    def exp_copy(j):
        return remote(exp_out.at[j], exp_in.at[h], exp_send.at[j], exp_recv.at[h], r, j)

    def exp_arrival(j):
        return remote(exp_out.at[j], exp_in.at[j], exp_send.at[j], exp_recv.at[j], r, j)

    for j in range(N):
        exp_out[j] = dot(hidden, down_v[0, :, pl.ds(j * columns, columns)]).astype(jnp.bfloat16)

        @pl.when(h != j)
        def _():
            exp_copy(j).start()

        @pl.when(h == j)
        def _():
            exp_in[j] = exp_out[j]

    line = lax.broadcasted_iota(jnp.int32, (ROWS, ALL), 1)
    want = lax.broadcasted_iota(jnp.int32, (ROWS, ALL), 0) + r * ROWS
    pick = jnp.where(line == want, 1.0, 0.0).astype(jnp.bfloat16)
    mine = jnp.concatenate([mid_all[h, j][:, : WIDTHS[j]] for j in range(N)], axis=1)
    own_mid = dot(pick, mine)
    top = ids.shape[0]
    packed = (ALL, PIECE)
    place = lax.broadcasted_iota(jnp.int32, packed, 0) % ROWS

    def spread_rows(read):
        result = jnp.full(packed, read(0))
        for i in range(1, ROWS):
            result = jnp.where(place == i, read(i), result)
        return result

    scored = [spread_rows(lambda i, k=k: routes[k, i]) for k in range(top)]
    named = [spread_rows(lambda i, k=k: ids[k, i]) for k in range(top)]
    whole = sum(scored[1:], scored[0])
    shares = [(s / whole).astype(jnp.bfloat16).astype(jnp.float32) for s in scored]
    weights = [
        sum(jnp.where(named[k] == e, shares[k], 0.0) for k in range(top)) for e in range(N)
    ]

    for j in range(N):

        @pl.when(h != j)
        def _():
            exp_arrival(j).wait_recv()

    expert = exp_in[0].astype(jnp.float32)
    for j in range(1, N):
        expert = expert + exp_in[j].astype(jnp.float32)

    def back_copy(i):
        return remote(back_out.at[i], back_in.at[r], back_send.at[i], back_recv.at[r], i, h)

    def back_arrival(i):
        return remote(back_out.at[i], back_in.at[i], back_send.at[i], back_recv.at[i], i, h)

    for i in range(N):
        back_out[i] = pack_rows(expert[ROWS * i : ROWS * (i + 1)]).astype(jnp.bfloat16)

        @pl.when(r != i)
        def _():
            back_copy(i).start()

        @pl.when(r == i)
        def _():
            back_in[i] = back_out[i]

    for i in range(N):

        @pl.when(r != i)
        def _():
            back_arrival(i).wait_recv()

    mixed = weights[0] * back_in[0].astype(jnp.float32)
    for e in range(1, N):
        mixed = mixed + weights[e] * back_in[e].astype(jnp.float32)
    skipped = by_row((ROWS, columns), 1, lambda i: skips[i])
    out[...] = jnp.where(skipped == 0, own_mid + unpack_rows(mixed), res).astype(jnp.bfloat16)

    for i in range(N):

        @pl.when(r != i)
        def _():
            att_copy(i).wait_send()
            mid_copy(i).wait_send()
            back_copy(i).wait_send()

        @pl.when(h != i)
        def _():
            proj_copy(i).wait_send()
            exp_copy(i).wait_send()

        mid_across(i).wait_send()
        mid_beside(i, 0).wait_send()
        mid_beside(i, 1).wait_send()

    @pl.when(r != h)
    def _():
        res_copy().wait_send()


def fused_device(
    residual,
    queries,
    cache_keys,
    cache_values,
    new_keys,
    new_values,
    cache_lengths,
    out_proj,
    norm_gain,
    skip_flags,
    expert_ids,
    route_scores,
    gate_w,
    up_w,
    down_w,
):
    bf16, f32 = jnp.bfloat16, jnp.float32
    gain = norm_gain[None, :]
    inputs = (
        queries,
        cache_keys,
        cache_values,
        new_keys,
        new_values,
        residual,
        out_proj,
        gain,
        gate_w,
        up_w,
        down_w,
    )
    scalars = (cache_lengths, skip_flags, expert_ids.T, route_scores.T)
    heads = queries.shape[1]
    columns = residual.shape[1]
    depth = heads * HEAD_SIZE // N
    dma = pltpu.SemaphoreType.DMA
    return pl.pallas_call(
        fused_kernel,
        out_shape=jax.ShapeDtypeStruct(residual.shape, bf16),
        in_specs=[pl.BlockSpec(memory_space=pl.ANY)] * (len(inputs) + len(scalars)),
        out_specs=pl.BlockSpec(memory_space=pltpu.VMEM),
        scratch_shapes=[pltpu.VMEM(x.shape, x.dtype) for x in inputs]
        + [pltpu.SMEM(x.shape, x.dtype) for x in scalars]
        + [
            pltpu.VMEM((ROWS * heads, HEAD_SIZE), f32),
            pltpu.VMEM((N, ALL, depth), bf16),
            pltpu.VMEM((depth // HEAD_SIZE, N * ALL, HEAD_SIZE), f32),
            pltpu.VMEM((ALL, PIECE), bf16),
            pltpu.VMEM((N, ALL, PIECE), bf16),
            pltpu.VMEM((N, ALL, PIECE), bf16),
            pltpu.VMEM((N, ALL, PIECE), bf16),
            pltpu.VMEM((N, N, ALL, PIECE), bf16),
            pltpu.VMEM((N, ALL, columns), bf16),
            pltpu.VMEM((N, ALL, columns), bf16),
            pltpu.VMEM((N, ALL, PIECE), bf16),
            pltpu.VMEM((N, ALL, PIECE), bf16),
            dma((len(inputs) + len(scalars) - 1,)),
            dma((N,)),
            dma((N,)),
            dma((N,)),
            dma,
            dma((N,)),
            dma((N,)),
            dma((N,)),
            dma((N,)),
            dma((N,)),
            dma((N, 2)),
            dma((N, N)),
            dma((N,)),
            dma((N,)),
            dma((N,)),
            dma((N,)),
        ],
        compiler_params=pltpu.CompilerParams(
            collective_id=0, has_side_effects=True, vmem_limit_bytes=63 * 1024 * 1024
        ),
    )(*inputs, *scalars)


def solution(mesh):
    return jax.shard_map(
        fused_device if fits_fused(mesh) else per_device,
        mesh=mesh,
        in_specs=(
            P(("groups", "rep"), "head"),
            P(("groups", "rep"), "head", None),
            P(("groups", "rep"), "head", None, None),
            P(("groups", "rep"), "head", None, None),
            P(("groups", "rep"), "head", None),
            P(("groups", "rep"), "head", None),
            P(("groups", "rep")),
            P("head", "rep"),
            P(),
            P(("groups", "rep")),
            P(("groups", "rep"), None),
            P(("groups", "rep"), None),
            P("rep", None, "head"),
            P("rep", None, "head"),
            P("rep", "head", None),
        ),
        out_specs=P(("groups", "rep"), "head"),
        check_vma=False,
    )
```

```python
import math

import jax
import jax.numpy as jnp
from jax import lax
from jax.experimental import pallas as pl
from jax.experimental.pallas import tpu as pltpu
from jax.sharding import PartitionSpec as P

D = 5120
CAP = 2


def hidden_block(arrivals, gate_w, up_w):
    gate_part = jnp.einsum("secd,edf->secf", arrivals, gate_w, preferred_element_type=jnp.float32)
    up_part = jnp.einsum("secd,edf->secf", arrivals, up_w, preferred_element_type=jnp.float32)
    return (jax.nn.silu(gate_part) * up_part).astype(jnp.bfloat16)


def per_device(
    residual,
    queries,
    cache_keys,
    cache_values,
    new_keys,
    new_values,
    cache_lengths,
    out_proj,
    norm_gain,
    skip_flags,
    expert_ids,
    route_scores,
    gate_w,
    up_w,
    down_w,
):
    rep_count = lax.axis_size("rep")
    local_rows = residual.shape[0]
    column_block = residual.shape[1]
    kv_local = cache_keys.shape[1]
    head_local = queries.shape[1]
    head_size = queries.shape[2]
    scaling = 1.0 / math.sqrt(head_size)
    grouped = queries.reshape(local_rows, kv_local, head_local // kv_local, head_size)
    scores = (
        jnp.einsum("rkgd,rkpd->rkgp", grouped, cache_keys, preferred_element_type=jnp.float32)
        * scaling
    )
    own_score = (
        jnp.einsum("rkgd,rkd->rkg", grouped, new_keys, preferred_element_type=jnp.float32) * scaling
    )
    filled = jnp.arange(cache_keys.shape[2], dtype=jnp.int32)[None, :] < cache_lengths[:, None]
    scores = jnp.where(filled[:, None, None, :], scores, -jnp.inf)
    highest = jnp.maximum(jnp.max(scores, axis=-1), own_score)
    powers = jnp.exp(scores - highest[..., None])
    own_power = jnp.exp(own_score - highest)
    denominator = jnp.sum(powers, axis=-1) + own_power
    probs = (powers / denominator[..., None]).astype(jnp.bfloat16)
    own_prob = (own_power / denominator).astype(jnp.bfloat16)
    attended = jnp.einsum(
        "rkgp,rkpd->rkgd", probs, cache_values, preferred_element_type=jnp.float32
    )
    attended = (
        attended
        + own_prob.astype(jnp.float32)[..., None] * new_values.astype(jnp.float32)[:, :, None, :]
    )
    attended = attended.astype(jnp.bfloat16).reshape(local_rows, head_local * head_size)
    partial_cols = jnp.dot(
        lax.all_gather(attended, "rep", axis=0, tiled=True),
        out_proj,
        preferred_element_type=jnp.float32,
    )
    regrouped = lax.all_to_all(
        partial_cols.astype(jnp.bfloat16), "rep", split_axis=0, concat_axis=1, tiled=True
    ).astype(partial_cols.dtype)
    projected = lax.psum_scatter(
        regrouped.astype(jnp.bfloat16), "head", scatter_dimension=1, tiled=True
    ).astype(jnp.float32)
    middle = (residual.astype(jnp.float32) + projected).astype(jnp.bfloat16)
    middle_wide = middle.astype(jnp.float32)
    exp_local = gate_w.shape[0]
    experts_all = rep_count * exp_local
    slot_count = experts_all * CAP
    top_count = expert_ids.shape[1]
    live = skip_flags == 0
    choose = (
        (expert_ids[:, :, None] == jnp.arange(experts_all, dtype=jnp.int32)[None, None, :])
        & live[:, None, None]
    ).astype(jnp.int32)
    flat_hits = choose.reshape(local_rows * top_count, experts_all)
    before = jnp.cumsum(flat_hits, axis=0) - flat_hits
    rank = jnp.sum(before * flat_hits, axis=1).reshape(local_rows, top_count)
    target = jnp.where(live[:, None], expert_ids * CAP + rank, -1)
    marks = (target[:, :, None] == jnp.arange(slot_count, dtype=jnp.int32)[None, None, :]).astype(
        jnp.float32
    )
    placing = jnp.sum(marks, axis=1).astype(jnp.bfloat16)
    shares = (route_scores / jnp.sum(route_scores, axis=1, keepdims=True)).astype(jnp.bfloat16)
    combine = jnp.sum(marks * shares.astype(jnp.float32)[:, :, None], axis=1).astype(jnp.bfloat16)
    full_middle = lax.all_gather(middle, "head", axis=1, tiled=True).astype(jnp.float32)
    mean_square = jnp.mean(full_middle * full_middle, axis=-1, keepdims=True)
    normed = (full_middle * lax.rsqrt(mean_square + 1e-05) * norm_gain[None, :]).astype(
        jnp.bfloat16
    )
    outgoing = jnp.einsum("rs,rd->sd", placing, normed, preferred_element_type=jnp.float32).astype(
        jnp.bfloat16
    )
    outgoing = outgoing.reshape(rep_count, exp_local, CAP, D)
    hidden = hidden_block(
        lax.all_to_all(outgoing, "rep", split_axis=0, concat_axis=0, tiled=True), gate_w, up_w
    )
    partial_out = jnp.einsum("secf,efd->secd", hidden, down_w, preferred_element_type=jnp.float32)
    summed = lax.psum_scatter(
        partial_out.astype(jnp.bfloat16), "head", scatter_dimension=3, tiled=True
    )
    expert_out = lax.all_to_all(summed, "rep", split_axis=0, concat_axis=0, tiled=True)
    expert_out = expert_out.reshape(slot_count, column_block)
    mixed = jnp.dot(combine, expert_out, preferred_element_type=jnp.float32)
    result = jnp.where(live[:, None], middle_wide + mixed, residual.astype(jnp.float32))
    return result.astype(jnp.bfloat16)


MESH = pl.DeviceIdType.MESH
N = 4
ROWS = 4
ALL = N * ROWS
HEAD_SIZE = 128
PIECE = 384
STARTS = (0, 384, 768, 1024)
WIDTHS = (384, 384, 256, 256)


def fits_fused(mesh):
    return mesh.shape["rep"] == N and mesh.shape["head"] == N


def pack_rows(x):
    pieces = []
    for start, width in zip(STARTS, WIDTHS):
        piece = x[:, start : start + width]
        if width < PIECE:
            piece = jnp.concatenate(
                [piece, jnp.zeros((x.shape[0], PIECE - width), x.dtype)], axis=1
            )
        pieces.append(piece)
    return jnp.concatenate(pieces, axis=0)


def unpack_rows(y):
    return jnp.concatenate(
        [y[ROWS * i : ROWS * (i + 1), :width] for i, width in enumerate(WIDTHS)], axis=1
    )


def by_row(shape, group, read):
    row = lax.broadcasted_iota(jnp.int32, shape, 0) // group
    out = jnp.full(shape, read(0))
    for i in range(1, shape[0] // group):
        out = jnp.where(row == i, read(i), out)
    return out


def dot(a, b):
    return jnp.dot(a, b, preferred_element_type=jnp.float32)


def fused_kernel(
    queries,
    cache_keys,
    cache_values,
    new_keys,
    new_values,
    residual,
    out_proj,
    norm_gain,
    gate_w,
    up_w,
    down_w,
    cache_lengths,
    skip_flags,
    expert_ids,
    route_scores,
    out,
    q_v,
    k_v,
    v_v,
    nk_v,
    nv_v,
    res_v,
    w_v,
    gain_v,
    gate_v,
    up_v,
    down_v,
    lengths,
    skips,
    ids,
    routes,
    att_f,
    att_all,
    att_wide,
    res_pack,
    res_in,
    proj_out,
    proj_in,
    mid_all,
    exp_out,
    exp_in,
    back_out,
    back_in,
    load_sem,
    w_sem,
    att_send,
    att_recv,
    res_send,
    res_recv,
    proj_send,
    proj_recv,
    mid_send,
    mid_recv,
    exp_send,
    exp_recv,
    back_send,
    back_recv,
):
    g = lax.axis_index("groups")
    r = lax.axis_index("rep")
    h = lax.axis_index("head")

    def remote(src, dst, send, recv, to_rep, to_head):
        return pltpu.make_async_remote_copy(
            src_ref=src,
            dst_ref=dst,
            send_sem=send,
            recv_sem=recv,
            device_id=(g, to_rep, to_head),
            device_id_type=MESH,
        )

    barrier = pltpu.get_barrier_semaphore()
    for turn in range(1, N * N):
        to_rep = lax.rem(r + turn // N, N)
        to_head = lax.rem(h + turn % N, N)
        pl.semaphore_signal(barrier, inc=1, device_id=(g, to_rep, to_head), device_id_type=MESH)

    loads = [
        pltpu.make_async_copy(src, dst, load_sem.at[i])
        for i, (src, dst) in enumerate(
            (
                (queries, q_v),
                (cache_keys, k_v),
                (new_keys, nk_v),
                (new_values, nv_v),
                (residual, res_v),
                (cache_values, v_v),
                (norm_gain, gain_v),
                (gate_w, gate_v),
                (up_w, up_v),
                (down_w, down_v),
                (cache_lengths, lengths),
                (skip_flags, skips),
                (expert_ids, ids),
                (route_scores, routes),
            )
        )
    ]
    depth = w_v.shape[0] // N
    w_loads = [
        pltpu.make_async_copy(
            out_proj.at[pl.ds(c * depth, depth)], w_v.at[pl.ds(c * depth, depth)], w_sem.at[c]
        )
        for c in range(N)
    ]
    for copy in loads[10:] + loads[:6] + w_loads + loads[6:10]:
        copy.start()

    heads = q_v.shape[1]
    kv = k_v.shape[1]
    lines = ROWS * heads
    blocks = ROWS * kv
    per_block = heads // kv
    scaling = 1.0 / math.sqrt(HEAD_SIZE)
    loads[0].wait()
    q = q_v[...].astype(jnp.float32).reshape(lines, HEAD_SIZE).astype(jnp.bfloat16)
    loads[1].wait()
    keys = k_v[...].reshape(blocks * k_v.shape[2], HEAD_SIZE)
    slots = k_v.shape[2]
    wide = lax.dot_general(
        q, keys, (((1,), (1,)), ((), ())), preferred_element_type=jnp.float32
    )
    block = lax.broadcasted_iota(jnp.int32, (lines, slots), 0) // per_block
    scores = wide[:, :slots]
    for t in range(1, blocks):
        scores = jnp.where(block == t, wide[:, t * slots : (t + 1) * slots], scores)
    scores = scores * scaling
    loads[2].wait()
    loads[3].wait()
    nk = jnp.concatenate([nk_v[i].astype(jnp.float32) for i in range(ROWS)], axis=0)
    nv = jnp.concatenate([nv_v[i].astype(jnp.float32) for i in range(ROWS)], axis=0)
    own_wide = lax.dot_general(
        q, nk.astype(jnp.bfloat16), (((1,), (1,)), ((), ())), preferred_element_type=jnp.float32
    )
    own_here = lax.broadcasted_iota(
        jnp.int32, (lines, blocks), 0
    ) // per_block == lax.broadcasted_iota(jnp.int32, (lines, blocks), 1)
    own = jnp.sum(jnp.where(own_here, own_wide, 0.0), axis=1, keepdims=True) * scaling
    for copy in loads[10:]:
        copy.wait()
    filled = lax.broadcasted_iota(jnp.int32, (lines, slots), 1) < by_row(
        (lines, slots), heads, lambda i: lengths[i]
    )
    scores = jnp.where(filled, scores, -jnp.inf)
    highest = jnp.maximum(jnp.max(scores, axis=1, keepdims=True), own)
    powers = jnp.exp(scores - highest)
    own_power = jnp.exp(own - highest)
    denominator = jnp.sum(powers, axis=1, keepdims=True) + own_power
    probs = powers / denominator
    own_prob = own_power / denominator
    spread = jnp.concatenate(
        [jnp.where(block == t, probs, 0.0).astype(jnp.bfloat16) for t in range(blocks)], axis=1
    )
    own_spread = jnp.where(own_here, own_prob, 0.0).astype(jnp.bfloat16)
    loads[5].wait()
    att = dot(spread, v_v[...].reshape(blocks * slots, HEAD_SIZE))
    att_f[...] = att + dot(own_spread, nv.astype(jnp.bfloat16))
    per_quarter = heads // N
    att_all[r] = jnp.concatenate(
        [att_f[pl.ds(j, ALL, stride=per_quarter), :] for j in range(per_quarter)], axis=1
    ).astype(jnp.bfloat16)
    loads[4].wait()
    res = res_v[...].astype(jnp.float32)
    res_pack[...] = pack_rows(res).astype(jnp.bfloat16)

    pl.semaphore_wait(barrier, N * N - 1)

    def att_copy(i):
        return remote(att_all.at[r], att_all.at[r], att_send.at[i], att_recv.at[r], i, h)

    def att_arrival(i):
        return remote(att_all.at[i], att_all.at[i], att_send.at[i], att_recv.at[i], i, h)

    def res_copy():
        return remote(res_pack, res_in.at[r], res_send, res_recv.at[r], h, h)

    def res_arrival(i):
        return remote(res_pack, res_in.at[i], res_send, res_recv.at[i], i, h)

    for i in range(N):

        @pl.when(r != i)
        def _():
            att_copy(i).start()

    @pl.when(r != h)
    def _():
        res_copy().start()

    @pl.when(r == h)
    def _():
        res_in[r] = res_pack[...]

    for i in range(N):

        @pl.when(r != i)
        def _():
            att_arrival(i).wait_recv()

    for t in range(per_quarter):
        cut = att_all[:, :, t * HEAD_SIZE : (t + 1) * HEAD_SIZE]
        att_wide[t] = cut.astype(jnp.float32).reshape(N * ALL, HEAD_SIZE)
    @pl.when(r == h)
    def _():
        for i in range(N):

            @pl.when(r != i)
            def _():
                res_arrival(i).wait_recv()

    @pl.when(r != h)
    def _():
        res_in[...] = jnp.zeros_like(res_in)

    total = jnp.concatenate(
        [unpack_rows(res_in[i].astype(jnp.float32)) for i in range(N)], axis=0
    )
    for c in range(N):
        w_loads[c].wait()
        lhs = jnp.concatenate(
            [att_wide[t, pl.ds(c, ALL, stride=N), :] for t in range(per_quarter)], axis=1
        ).astype(jnp.bfloat16)
        part = dot(lhs, w_v[pl.ds(c * depth, depth), :])
        total = total + part

    def proj_copy(j):
        return remote(proj_out.at[j], proj_in.at[h], proj_send.at[j], proj_recv.at[h], r, j)

    def proj_arrival(j):
        return remote(proj_out.at[j], proj_in.at[j], proj_send.at[j], proj_recv.at[j], r, j)

    for j in range(N):
        piece = total[:, STARTS[j] : STARTS[j] + WIDTHS[j]].astype(jnp.bfloat16)
        proj_out[j, :, : WIDTHS[j]] = piece
        if WIDTHS[j] < PIECE:
            proj_out[j, :, WIDTHS[j] :] = jnp.zeros((ALL, PIECE - WIDTHS[j]), jnp.bfloat16)

        @pl.when(h != j)
        def _():
            proj_copy(j).start()

        @pl.when(h == j)
        def _():
            proj_in[j] = proj_out[j]

    for j in range(N):

        @pl.when(h != j)
        def _():
            proj_arrival(j).wait_recv()

    summed = proj_in[0].astype(jnp.float32)
    for j in range(1, N):
        summed = summed + proj_in[j].astype(jnp.float32)
    mid_all[r, h] = summed.astype(jnp.bfloat16)

    def partner(turn):
        return lax.rem(r + turn // N, N), lax.rem(h + turn % N, N)

    def mid_copy(turn):
        i, j = partner(turn)
        return remote(
            mid_all.at[r, h], mid_all.at[r, h], mid_send.at[turn], mid_recv.at[r, h], i, j
        )

    def mid_arrival(turn):
        i, j = partner(turn)
        return remote(
            mid_all.at[i, j], mid_all.at[i, j], mid_send.at[turn], mid_recv.at[i, j], i, j
        )

    order = [N * i + j for i in (2, 1, 3, 0) for j in range(N) if i or j]
    for turn in order:
        mid_copy(turn).start()
    for i in range(6, 10):
        loads[i].wait()
    for turn in range(1, N * N):
        mid_arrival(turn).wait_recv()

    rows = []
    squares = jnp.zeros((ALL, 1), jnp.float32)
    for i in range(N):
        x = jnp.concatenate([mid_all[i, j][:, : WIDTHS[j]] for j in range(N)], axis=1).astype(
            jnp.float32
        )
        rows.append(x)
        squares = squares + jnp.sum(x * x, axis=1, keepdims=True)
    columns = rows[0].shape[1]
    scale = lax.rsqrt(squares * (1.0 / (N * columns)) + 1e-05)
    gate = jnp.zeros((ALL, gate_v.shape[2]), jnp.float32)
    up = jnp.zeros((ALL, up_v.shape[2]), jnp.float32)
    for i in range(N):
        cut = pl.ds(i * columns, columns)
        normed = (rows[i] * scale * gain_v[:, cut]).astype(jnp.bfloat16)
        gate = gate + dot(normed, gate_v[0, cut, :])
        up = up + dot(normed, up_v[0, cut, :])
    hidden = (gate / (1.0 + jnp.exp(-gate)) * up).astype(jnp.bfloat16)

    def exp_copy(j):
        return remote(exp_out.at[j], exp_in.at[h], exp_send.at[j], exp_recv.at[h], r, j)

    def exp_arrival(j):
        return remote(exp_out.at[j], exp_in.at[j], exp_send.at[j], exp_recv.at[j], r, j)

    for j in range(N):
        exp_out[j] = dot(hidden, down_v[0, :, pl.ds(j * columns, columns)]).astype(jnp.bfloat16)

        @pl.when(h != j)
        def _():
            exp_copy(j).start()

        @pl.when(h == j)
        def _():
            exp_in[j] = exp_out[j]

    line = lax.broadcasted_iota(jnp.int32, (ROWS, ALL), 1)
    want = lax.broadcasted_iota(jnp.int32, (ROWS, ALL), 0) + r * ROWS
    pick = jnp.where(line == want, 1.0, 0.0).astype(jnp.bfloat16)
    mine = jnp.concatenate([mid_all[h, j][:, : WIDTHS[j]] for j in range(N)], axis=1)
    own_mid = dot(pick, mine)
    top = ids.shape[0]
    packed = (ALL, PIECE)
    place = lax.broadcasted_iota(jnp.int32, packed, 0) % ROWS

    def spread_rows(read):
        result = jnp.full(packed, read(0))
        for i in range(1, ROWS):
            result = jnp.where(place == i, read(i), result)
        return result

    scored = [spread_rows(lambda i, k=k: routes[k, i]) for k in range(top)]
    named = [spread_rows(lambda i, k=k: ids[k, i]) for k in range(top)]
    whole = sum(scored[1:], scored[0])
    shares = [(s / whole).astype(jnp.bfloat16).astype(jnp.float32) for s in scored]
    weights = [
        sum(jnp.where(named[k] == e, shares[k], 0.0) for k in range(top)) for e in range(N)
    ]

    for j in range(N):

        @pl.when(h != j)
        def _():
            exp_arrival(j).wait_recv()

    expert = exp_in[0].astype(jnp.float32)
    for j in range(1, N):
        expert = expert + exp_in[j].astype(jnp.float32)

    def back_copy(i):
        return remote(back_out.at[i], back_in.at[r], back_send.at[i], back_recv.at[r], i, h)

    def back_arrival(i):
        return remote(back_out.at[i], back_in.at[i], back_send.at[i], back_recv.at[i], i, h)

    for i in range(N):
        back_out[i] = pack_rows(expert[ROWS * i : ROWS * (i + 1)]).astype(jnp.bfloat16)

        @pl.when(r != i)
        def _():
            back_copy(i).start()

        @pl.when(r == i)
        def _():
            back_in[i] = back_out[i]

    for i in range(N):

        @pl.when(r != i)
        def _():
            back_arrival(i).wait_recv()

    mixed = weights[0] * back_in[0].astype(jnp.float32)
    for e in range(1, N):
        mixed = mixed + weights[e] * back_in[e].astype(jnp.float32)
    skipped = by_row((ROWS, columns), 1, lambda i: skips[i])
    out[...] = jnp.where(skipped == 0, own_mid + unpack_rows(mixed), res).astype(jnp.bfloat16)

    for i in range(N):

        @pl.when(r != i)
        def _():
            att_copy(i).wait_send()
            back_copy(i).wait_send()

        @pl.when(h != i)
        def _():
            proj_copy(i).wait_send()
            exp_copy(i).wait_send()

    for turn in range(1, N * N):
        mid_copy(turn).wait_send()
    @pl.when(r != h)
    def _():
        res_copy().wait_send()


def fused_device(
    residual,
    queries,
    cache_keys,
    cache_values,
    new_keys,
    new_values,
    cache_lengths,
    out_proj,
    norm_gain,
    skip_flags,
    expert_ids,
    route_scores,
    gate_w,
    up_w,
    down_w,
):
    bf16, f32 = jnp.bfloat16, jnp.float32
    gain = norm_gain[None, :]
    inputs = (
        queries,
        cache_keys,
        cache_values,
        new_keys,
        new_values,
        residual,
        out_proj,
        gain,
        gate_w,
        up_w,
        down_w,
    )
    scalars = (cache_lengths, skip_flags, expert_ids.T, route_scores.T)
    heads = queries.shape[1]
    columns = residual.shape[1]
    depth = heads * HEAD_SIZE // N
    dma = pltpu.SemaphoreType.DMA
    return pl.pallas_call(
        fused_kernel,
        out_shape=jax.ShapeDtypeStruct(residual.shape, bf16),
        in_specs=[pl.BlockSpec(memory_space=pl.ANY)] * (len(inputs) + len(scalars)),
        out_specs=pl.BlockSpec(memory_space=pltpu.VMEM),
        scratch_shapes=[pltpu.VMEM(x.shape, x.dtype) for x in inputs]
        + [pltpu.SMEM(x.shape, x.dtype) for x in scalars]
        + [
            pltpu.VMEM((ROWS * heads, HEAD_SIZE), f32),
            pltpu.VMEM((N, ALL, depth), bf16),
            pltpu.VMEM((depth // HEAD_SIZE, N * ALL, HEAD_SIZE), f32),
            pltpu.VMEM((ALL, PIECE), bf16),
            pltpu.VMEM((N, ALL, PIECE), bf16),
            pltpu.VMEM((N, ALL, PIECE), bf16),
            pltpu.VMEM((N, ALL, PIECE), bf16),
            pltpu.VMEM((N, N, ALL, PIECE), bf16),
            pltpu.VMEM((N, ALL, columns), bf16),
            pltpu.VMEM((N, ALL, columns), bf16),
            pltpu.VMEM((N, ALL, PIECE), bf16),
            pltpu.VMEM((N, ALL, PIECE), bf16),
            dma((len(inputs) + len(scalars) - 1,)),
            dma((N,)),
            dma((N,)),
            dma((N,)),
            dma,
            dma((N,)),
            dma((N,)),
            dma((N,)),
            dma((N * N,)),
            dma((N, N)),
            dma((N,)),
            dma((N,)),
            dma((N,)),
            dma((N,)),
        ],
        compiler_params=pltpu.CompilerParams(
            collective_id=0, has_side_effects=True, vmem_limit_bytes=63 * 1024 * 1024
        ),
    )(*inputs, *scalars)


def solution(mesh):
    return jax.shard_map(
        fused_device if fits_fused(mesh) else per_device,
        mesh=mesh,
        in_specs=(
            P(("groups", "rep"), "head"),
            P(("groups", "rep"), "head", None),
            P(("groups", "rep"), "head", None, None),
            P(("groups", "rep"), "head", None, None),
            P(("groups", "rep"), "head", None),
            P(("groups", "rep"), "head", None),
            P(("groups", "rep")),
            P("head", "rep"),
            P(),
            P(("groups", "rep")),
            P(("groups", "rep"), None),
            P(("groups", "rep"), None),
            P("rep", None, "head"),
            P("rep", None, "head"),
            P("rep", "head", None),
        ),
        out_specs=P(("groups", "rep"), "head"),
        check_vma=False,
    )
```

```python
import math

import jax
import jax.numpy as jnp
from jax import lax
from jax.experimental import pallas as pl
from jax.experimental.pallas import tpu as pltpu
from jax.sharding import PartitionSpec as P

D = 5120
CAP = 2


def hidden_block(arrivals, gate_w, up_w):
    gate_part = jnp.einsum("secd,edf->secf", arrivals, gate_w, preferred_element_type=jnp.float32)
    up_part = jnp.einsum("secd,edf->secf", arrivals, up_w, preferred_element_type=jnp.float32)
    return (jax.nn.silu(gate_part) * up_part).astype(jnp.bfloat16)


def per_device(
    residual,
    queries,
    cache_keys,
    cache_values,
    new_keys,
    new_values,
    cache_lengths,
    out_proj,
    norm_gain,
    skip_flags,
    expert_ids,
    route_scores,
    gate_w,
    up_w,
    down_w,
):
    rep_count = lax.axis_size("rep")
    local_rows = residual.shape[0]
    column_block = residual.shape[1]
    kv_local = cache_keys.shape[1]
    head_local = queries.shape[1]
    head_size = queries.shape[2]
    scaling = 1.0 / math.sqrt(head_size)
    grouped = queries.reshape(local_rows, kv_local, head_local // kv_local, head_size)
    scores = (
        jnp.einsum("rkgd,rkpd->rkgp", grouped, cache_keys, preferred_element_type=jnp.float32)
        * scaling
    )
    own_score = (
        jnp.einsum("rkgd,rkd->rkg", grouped, new_keys, preferred_element_type=jnp.float32) * scaling
    )
    filled = jnp.arange(cache_keys.shape[2], dtype=jnp.int32)[None, :] < cache_lengths[:, None]
    scores = jnp.where(filled[:, None, None, :], scores, -jnp.inf)
    highest = jnp.maximum(jnp.max(scores, axis=-1), own_score)
    powers = jnp.exp(scores - highest[..., None])
    own_power = jnp.exp(own_score - highest)
    denominator = jnp.sum(powers, axis=-1) + own_power
    probs = (powers / denominator[..., None]).astype(jnp.bfloat16)
    own_prob = (own_power / denominator).astype(jnp.bfloat16)
    attended = jnp.einsum(
        "rkgp,rkpd->rkgd", probs, cache_values, preferred_element_type=jnp.float32
    )
    attended = (
        attended
        + own_prob.astype(jnp.float32)[..., None] * new_values.astype(jnp.float32)[:, :, None, :]
    )
    attended = attended.astype(jnp.bfloat16).reshape(local_rows, head_local * head_size)
    partial_cols = jnp.dot(
        lax.all_gather(attended, "rep", axis=0, tiled=True),
        out_proj,
        preferred_element_type=jnp.float32,
    )
    regrouped = lax.all_to_all(
        partial_cols.astype(jnp.bfloat16), "rep", split_axis=0, concat_axis=1, tiled=True
    ).astype(partial_cols.dtype)
    projected = lax.psum_scatter(
        regrouped.astype(jnp.bfloat16), "head", scatter_dimension=1, tiled=True
    ).astype(jnp.float32)
    middle = (residual.astype(jnp.float32) + projected).astype(jnp.bfloat16)
    middle_wide = middle.astype(jnp.float32)
    exp_local = gate_w.shape[0]
    experts_all = rep_count * exp_local
    slot_count = experts_all * CAP
    top_count = expert_ids.shape[1]
    live = skip_flags == 0
    choose = (
        (expert_ids[:, :, None] == jnp.arange(experts_all, dtype=jnp.int32)[None, None, :])
        & live[:, None, None]
    ).astype(jnp.int32)
    flat_hits = choose.reshape(local_rows * top_count, experts_all)
    before = jnp.cumsum(flat_hits, axis=0) - flat_hits
    rank = jnp.sum(before * flat_hits, axis=1).reshape(local_rows, top_count)
    target = jnp.where(live[:, None], expert_ids * CAP + rank, -1)
    marks = (target[:, :, None] == jnp.arange(slot_count, dtype=jnp.int32)[None, None, :]).astype(
        jnp.float32
    )
    placing = jnp.sum(marks, axis=1).astype(jnp.bfloat16)
    shares = (route_scores / jnp.sum(route_scores, axis=1, keepdims=True)).astype(jnp.bfloat16)
    combine = jnp.sum(marks * shares.astype(jnp.float32)[:, :, None], axis=1).astype(jnp.bfloat16)
    full_middle = lax.all_gather(middle, "head", axis=1, tiled=True).astype(jnp.float32)
    mean_square = jnp.mean(full_middle * full_middle, axis=-1, keepdims=True)
    normed = (full_middle * lax.rsqrt(mean_square + 1e-05) * norm_gain[None, :]).astype(
        jnp.bfloat16
    )
    outgoing = jnp.einsum("rs,rd->sd", placing, normed, preferred_element_type=jnp.float32).astype(
        jnp.bfloat16
    )
    outgoing = outgoing.reshape(rep_count, exp_local, CAP, D)
    hidden = hidden_block(
        lax.all_to_all(outgoing, "rep", split_axis=0, concat_axis=0, tiled=True), gate_w, up_w
    )
    partial_out = jnp.einsum("secf,efd->secd", hidden, down_w, preferred_element_type=jnp.float32)
    summed = lax.psum_scatter(
        partial_out.astype(jnp.bfloat16), "head", scatter_dimension=3, tiled=True
    )
    expert_out = lax.all_to_all(summed, "rep", split_axis=0, concat_axis=0, tiled=True)
    expert_out = expert_out.reshape(slot_count, column_block)
    mixed = jnp.dot(combine, expert_out, preferred_element_type=jnp.float32)
    result = jnp.where(live[:, None], middle_wide + mixed, residual.astype(jnp.float32))
    return result.astype(jnp.bfloat16)


MESH = pl.DeviceIdType.MESH
N = 4
ROWS = 4
ALL = N * ROWS
HEAD_SIZE = 128
PIECE = 384
STARTS = (0, 384, 768, 1024)
WIDTHS = (384, 384, 256, 256)


def fits_fused(mesh):
    return mesh.shape["rep"] == N and mesh.shape["head"] == N


def pack_rows(x):
    pieces = []
    for start, width in zip(STARTS, WIDTHS):
        piece = x[:, start : start + width]
        if width < PIECE:
            piece = jnp.concatenate(
                [piece, jnp.zeros((x.shape[0], PIECE - width), x.dtype)], axis=1
            )
        pieces.append(piece)
    return jnp.concatenate(pieces, axis=0)


def unpack_rows(y):
    return jnp.concatenate(
        [y[ROWS * i : ROWS * (i + 1), :width] for i, width in enumerate(WIDTHS)], axis=1
    )


def by_row(shape, group, read):
    row = lax.broadcasted_iota(jnp.int32, shape, 0) // group
    out = jnp.full(shape, read(0))
    for i in range(1, shape[0] // group):
        out = jnp.where(row == i, read(i), out)
    return out


def dot(a, b):
    return jnp.dot(a, b, preferred_element_type=jnp.float32)


def fused_kernel(
    queries,
    cache_keys,
    cache_values,
    new_keys,
    new_values,
    residual,
    out_proj,
    norm_gain,
    gate_w,
    up_w,
    down_w,
    cache_lengths,
    skip_flags,
    expert_ids,
    route_scores,
    out,
    q_v,
    k_v,
    v_v,
    nk_v,
    nv_v,
    res_v,
    w_v,
    gain_v,
    gate_v,
    up_v,
    down_v,
    lengths,
    skips,
    ids,
    routes,
    att_f,
    att_all,
    att_wide,
    res_pack,
    res_in,
    proj_out,
    proj_in,
    mid_all,
    back_out,
    back_in,
    load_sem,
    w_sem,
    att_send,
    att_recv,
    res_send,
    res_recv,
    proj_send,
    proj_recv,
    mid_send,
    mid_recv,
    back_send,
    back_recv,
):
    g = lax.axis_index("groups")
    r = lax.axis_index("rep")
    h = lax.axis_index("head")

    def remote(src, dst, send, recv, to_rep, to_head):
        return pltpu.make_async_remote_copy(
            src_ref=src,
            dst_ref=dst,
            send_sem=send,
            recv_sem=recv,
            device_id=(g, to_rep, to_head),
            device_id_type=MESH,
        )

    barrier = pltpu.get_barrier_semaphore()
    for turn in range(1, N * N):
        to_rep = lax.rem(r + turn // N, N)
        to_head = lax.rem(h + turn % N, N)
        pl.semaphore_signal(barrier, inc=1, device_id=(g, to_rep, to_head), device_id_type=MESH)

    loads = [
        pltpu.make_async_copy(src, dst, load_sem.at[i])
        for i, (src, dst) in enumerate(
            (
                (queries, q_v),
                (cache_keys, k_v),
                (new_keys, nk_v),
                (new_values, nv_v),
                (residual, res_v),
                (cache_values, v_v),
                (norm_gain, gain_v),
                (gate_w, gate_v),
                (up_w, up_v),
                (down_w, down_v),
                (cache_lengths, lengths),
                (skip_flags, skips),
                (expert_ids, ids),
                (route_scores, routes),
            )
        )
    ]
    depth = w_v.shape[0] // N
    w_loads = [
        pltpu.make_async_copy(
            out_proj.at[pl.ds(c * depth, depth)], w_v.at[pl.ds(c * depth, depth)], w_sem.at[c]
        )
        for c in range(N)
    ]
    for copy in loads[10:] + loads[:6] + w_loads + loads[6:10]:
        copy.start()

    heads = q_v.shape[1]
    kv = k_v.shape[1]
    lines = ROWS * heads
    blocks = ROWS * kv
    per_block = heads // kv
    scaling = 1.0 / math.sqrt(HEAD_SIZE)
    loads[0].wait()
    q = q_v[...].astype(jnp.float32).reshape(lines, HEAD_SIZE).astype(jnp.bfloat16)
    loads[1].wait()
    keys = k_v[...].reshape(blocks * k_v.shape[2], HEAD_SIZE)
    slots = k_v.shape[2]
    wide = lax.dot_general(
        q, keys, (((1,), (1,)), ((), ())), preferred_element_type=jnp.float32
    )
    block = lax.broadcasted_iota(jnp.int32, (lines, slots), 0) // per_block
    scores = wide[:, :slots]
    for t in range(1, blocks):
        scores = jnp.where(block == t, wide[:, t * slots : (t + 1) * slots], scores)
    scores = scores * scaling
    loads[2].wait()
    loads[3].wait()
    nk = jnp.concatenate([nk_v[i].astype(jnp.float32) for i in range(ROWS)], axis=0)
    nv = jnp.concatenate([nv_v[i].astype(jnp.float32) for i in range(ROWS)], axis=0)
    own_wide = lax.dot_general(
        q, nk.astype(jnp.bfloat16), (((1,), (1,)), ((), ())), preferred_element_type=jnp.float32
    )
    own_here = lax.broadcasted_iota(
        jnp.int32, (lines, blocks), 0
    ) // per_block == lax.broadcasted_iota(jnp.int32, (lines, blocks), 1)
    own = jnp.sum(jnp.where(own_here, own_wide, 0.0), axis=1, keepdims=True) * scaling
    for copy in loads[10:]:
        copy.wait()
    filled = lax.broadcasted_iota(jnp.int32, (lines, slots), 1) < by_row(
        (lines, slots), heads, lambda i: lengths[i]
    )
    scores = jnp.where(filled, scores, -jnp.inf)
    highest = jnp.maximum(jnp.max(scores, axis=1, keepdims=True), own)
    powers = jnp.exp(scores - highest)
    own_power = jnp.exp(own - highest)
    denominator = jnp.sum(powers, axis=1, keepdims=True) + own_power
    probs = powers / denominator
    own_prob = own_power / denominator
    spread = jnp.concatenate(
        [jnp.where(block == t, probs, 0.0).astype(jnp.bfloat16) for t in range(blocks)], axis=1
    )
    own_spread = jnp.where(own_here, own_prob, 0.0).astype(jnp.bfloat16)
    loads[5].wait()
    att = dot(spread, v_v[...].reshape(blocks * slots, HEAD_SIZE))
    att_f[...] = att + dot(own_spread, nv.astype(jnp.bfloat16))
    per_quarter = heads // N
    att_all[r] = jnp.concatenate(
        [att_f[pl.ds(j, ALL, stride=per_quarter), :] for j in range(per_quarter)], axis=1
    ).astype(jnp.bfloat16)
    loads[4].wait()
    res = res_v[...].astype(jnp.float32)
    res_pack[...] = pack_rows(res).astype(jnp.bfloat16)

    pl.semaphore_wait(barrier, N * N - 1)

    def att_copy(i):
        return remote(att_all.at[r], att_all.at[r], att_send.at[i], att_recv.at[r], i, h)

    def att_arrival(i):
        return remote(att_all.at[i], att_all.at[i], att_send.at[i], att_recv.at[i], i, h)

    def res_copy():
        return remote(res_pack, res_in.at[r], res_send, res_recv.at[r], h, h)

    def res_arrival(i):
        return remote(res_pack, res_in.at[i], res_send, res_recv.at[i], i, h)

    for i in range(N):

        @pl.when(r != i)
        def _():
            att_copy(i).start()

    @pl.when(r != h)
    def _():
        res_copy().start()

    @pl.when(r == h)
    def _():
        res_in[r] = res_pack[...]

    for i in range(N):

        @pl.when(r != i)
        def _():
            att_arrival(i).wait_recv()

    for t in range(per_quarter):
        cut = att_all[:, :, t * HEAD_SIZE : (t + 1) * HEAD_SIZE]
        att_wide[t] = cut.astype(jnp.float32).reshape(N * ALL, HEAD_SIZE)
    @pl.when(r == h)
    def _():
        for i in range(N):

            @pl.when(r != i)
            def _():
                res_arrival(i).wait_recv()

    @pl.when(r != h)
    def _():
        res_in[...] = jnp.zeros_like(res_in)

    total = jnp.concatenate(
        [unpack_rows(res_in[i].astype(jnp.float32)) for i in range(N)], axis=0
    )
    for c in range(N):
        w_loads[c].wait()
        lhs = jnp.concatenate(
            [att_wide[t, pl.ds(c, ALL, stride=N), :] for t in range(per_quarter)], axis=1
        ).astype(jnp.bfloat16)
        part = dot(lhs, w_v[pl.ds(c * depth, depth), :])
        total = total + part

    def proj_copy(j):
        return remote(proj_out.at[j], proj_in.at[h], proj_send.at[j], proj_recv.at[h], r, j)

    def proj_arrival(j):
        return remote(proj_out.at[j], proj_in.at[j], proj_send.at[j], proj_recv.at[j], r, j)

    for j in range(N):
        piece = total[:, STARTS[j] : STARTS[j] + WIDTHS[j]].astype(jnp.bfloat16)
        proj_out[j, :, : WIDTHS[j]] = piece
        if WIDTHS[j] < PIECE:
            proj_out[j, :, WIDTHS[j] :] = jnp.zeros((ALL, PIECE - WIDTHS[j]), jnp.bfloat16)

        @pl.when(h != j)
        def _():
            proj_copy(j).start()

        @pl.when(h == j)
        def _():
            proj_in[j] = proj_out[j]

    for j in range(N):

        @pl.when(h != j)
        def _():
            proj_arrival(j).wait_recv()

    summed = proj_in[0].astype(jnp.float32)
    for j in range(1, N):
        summed = summed + proj_in[j].astype(jnp.float32)
    mid_all[r, h] = summed.astype(jnp.bfloat16)

    def partner(turn):
        return lax.rem(r + turn // N, N), lax.rem(h + turn % N, N)

    def mid_copy(turn):
        i, j = partner(turn)
        return remote(
            mid_all.at[r, h], mid_all.at[r, h], mid_send.at[turn], mid_recv.at[r, h], i, j
        )

    def mid_arrival(turn):
        i, j = partner(turn)
        return remote(
            mid_all.at[i, j], mid_all.at[i, j], mid_send.at[turn], mid_recv.at[i, j], i, j
        )

    order = [N * i + j for i in (2, 1, 3, 0) for j in range(N) if i or j]
    for turn in order:
        mid_copy(turn).start()
    for i in range(6, 10):
        loads[i].wait()
    for turn in range(1, N * N):
        mid_arrival(turn).wait_recv()

    rows = []
    squares = jnp.zeros((ALL, 1), jnp.float32)
    for i in range(N):
        x = jnp.concatenate([mid_all[i, j][:, : WIDTHS[j]] for j in range(N)], axis=1).astype(
            jnp.float32
        )
        rows.append(x)
        squares = squares + jnp.sum(x * x, axis=1, keepdims=True)
    columns = rows[0].shape[1]
    scale = lax.rsqrt(squares * (1.0 / (N * columns)) + 1e-05)
    gate = jnp.zeros((ALL, gate_v.shape[2]), jnp.float32)
    up = jnp.zeros((ALL, up_v.shape[2]), jnp.float32)
    for i in range(N):
        cut = pl.ds(i * columns, columns)
        normed = (rows[i] * scale * gain_v[:, cut]).astype(jnp.bfloat16)
        gate = gate + dot(normed, gate_v[0, cut, :])
        up = up + dot(normed, up_v[0, cut, :])
    hidden = (gate / (1.0 + jnp.exp(-gate)) * up).astype(jnp.bfloat16)

    def back_copy(turn):
        i, j = partner(turn)
        return remote(
            back_out.at[i, j], back_in.at[r, h], back_send.at[turn], back_recv.at[r, h], i, j
        )

    def back_arrival(turn):
        i, j = partner(turn)
        return remote(
            back_out.at[i, j], back_in.at[i, j], back_send.at[turn], back_recv.at[i, j], i, j
        )

    for j in range(N):
        part = dot(hidden, down_v[0, :, pl.ds(j * columns, columns)])
        for i in range(N):
            back_out[i, j] = pack_rows(part[ROWS * i : ROWS * (i + 1)]).astype(jnp.bfloat16)
        turned = lax.rem(j - h + N, N)
        for away in (2, 1, 3, 0):
            i = lax.rem(r + away, N)
            copy = remote(
                back_out.at[i, j],
                back_in.at[r, h],
                back_send.at[away * N + turned],
                back_recv.at[r, h],
                i,
                j,
            )
            if away:
                copy.start()
            else:
                pl.when(h != j)(copy.start)
    back_in[r, h] = back_out[r, h]

    line = lax.broadcasted_iota(jnp.int32, (ROWS, ALL), 1)
    want = lax.broadcasted_iota(jnp.int32, (ROWS, ALL), 0) + r * ROWS
    pick = jnp.where(line == want, 1.0, 0.0).astype(jnp.bfloat16)
    mine = jnp.concatenate([mid_all[h, j][:, : WIDTHS[j]] for j in range(N)], axis=1)
    own_mid = dot(pick, mine)
    top = ids.shape[0]
    packed = (ALL, PIECE)
    place = lax.broadcasted_iota(jnp.int32, packed, 0) % ROWS

    def spread_rows(read):
        result = jnp.full(packed, read(0))
        for i in range(1, ROWS):
            result = jnp.where(place == i, read(i), result)
        return result

    scored = [spread_rows(lambda i, k=k: routes[k, i]) for k in range(top)]
    named = [spread_rows(lambda i, k=k: ids[k, i]) for k in range(top)]
    whole = sum(scored[1:], scored[0])
    shares = [(s / whole).astype(jnp.bfloat16).astype(jnp.float32) for s in scored]
    weights = [
        sum(jnp.where(named[k] == e, shares[k], 0.0) for k in range(top)) for e in range(N)
    ]

    for turn in range(1, N * N):
        back_arrival(turn).wait_recv()

    mixed = jnp.zeros(packed, jnp.float32)
    for e in range(N):
        expert = back_in[e, 0].astype(jnp.float32)
        for j in range(1, N):
            expert = expert + back_in[e, j].astype(jnp.float32)
        mixed = mixed + weights[e] * expert
    skipped = by_row((ROWS, columns), 1, lambda i: skips[i])
    out[...] = jnp.where(skipped == 0, own_mid + unpack_rows(mixed), res).astype(jnp.bfloat16)

    for i in range(N):

        @pl.when(r != i)
        def _():
            att_copy(i).wait_send()

        @pl.when(h != i)
        def _():
            proj_copy(i).wait_send()

    for turn in range(1, N * N):
        mid_copy(turn).wait_send()
        back_copy(turn).wait_send()
    @pl.when(r != h)
    def _():
        res_copy().wait_send()


def fused_device(
    residual,
    queries,
    cache_keys,
    cache_values,
    new_keys,
    new_values,
    cache_lengths,
    out_proj,
    norm_gain,
    skip_flags,
    expert_ids,
    route_scores,
    gate_w,
    up_w,
    down_w,
):
    bf16, f32 = jnp.bfloat16, jnp.float32
    gain = norm_gain[None, :]
    inputs = (
        queries,
        cache_keys,
        cache_values,
        new_keys,
        new_values,
        residual,
        out_proj,
        gain,
        gate_w,
        up_w,
        down_w,
    )
    scalars = (cache_lengths, skip_flags, expert_ids.T, route_scores.T)
    heads = queries.shape[1]
    columns = residual.shape[1]
    depth = heads * HEAD_SIZE // N
    dma = pltpu.SemaphoreType.DMA
    return pl.pallas_call(
        fused_kernel,
        out_shape=jax.ShapeDtypeStruct(residual.shape, bf16),
        in_specs=[pl.BlockSpec(memory_space=pl.ANY)] * (len(inputs) + len(scalars)),
        out_specs=pl.BlockSpec(memory_space=pltpu.VMEM),
        scratch_shapes=[pltpu.VMEM(x.shape, x.dtype) for x in inputs]
        + [pltpu.SMEM(x.shape, x.dtype) for x in scalars]
        + [
            pltpu.VMEM((ROWS * heads, HEAD_SIZE), f32),
            pltpu.VMEM((N, ALL, depth), bf16),
            pltpu.VMEM((depth // HEAD_SIZE, N * ALL, HEAD_SIZE), f32),
            pltpu.VMEM((ALL, PIECE), bf16),
            pltpu.VMEM((N, ALL, PIECE), bf16),
            pltpu.VMEM((N, ALL, PIECE), bf16),
            pltpu.VMEM((N, ALL, PIECE), bf16),
            pltpu.VMEM((N, N, ALL, PIECE), bf16),
            pltpu.VMEM((N, N, ALL, PIECE), bf16),
            pltpu.VMEM((N, N, ALL, PIECE), bf16),
            dma((len(inputs) + len(scalars) - 1,)),
            dma((N,)),
            dma((N,)),
            dma((N,)),
            dma,
            dma((N,)),
            dma((N,)),
            dma((N,)),
            dma((N * N,)),
            dma((N, N)),
            dma((N * N,)),
            dma((N, N)),
        ],
        compiler_params=pltpu.CompilerParams(
            collective_id=0, has_side_effects=True, vmem_limit_bytes=63 * 1024 * 1024
        ),
    )(*inputs, *scalars)


def solution(mesh):
    return jax.shard_map(
        fused_device if fits_fused(mesh) else per_device,
        mesh=mesh,
        in_specs=(
            P(("groups", "rep"), "head"),
            P(("groups", "rep"), "head", None),
            P(("groups", "rep"), "head", None, None),
            P(("groups", "rep"), "head", None, None),
            P(("groups", "rep"), "head", None),
            P(("groups", "rep"), "head", None),
            P(("groups", "rep")),
            P("head", "rep"),
            P(),
            P(("groups", "rep")),
            P(("groups", "rep"), None),
            P(("groups", "rep"), None),
            P("rep", None, "head"),
            P("rep", None, "head"),
            P("rep", "head", None),
        ),
        out_specs=P(("groups", "rep"), "head"),
        check_vma=False,
    )
```
